768 devices in a mesh: aa: 96 (over z, x, core), ba: 8 (over y).
Axes of the slice: x: 4, y: 8, z: 12, core: 2. Of those that a mesh axis runs over, the one named last changes fastest.
Arguments:
- prev_vector: float32 [4608, 6144], P('aa', 'ba'), may hold values from -6 to 6
- this_vector: float32 [4608, 6144], P('aa', 'ba'), may hold values from -6 to 6
- diagonal: float32 [4608, 6144], P('aa', 'ba'), may hold values from -0.5 to 0.5
- alpha_blocks: bfloat16 [36, 2, 128, 128], replicated, may hold values from -0.21875 to 0.21875
- alpha_classes: int32 [8], replicated, may hold values from 1 to 8, 36 in all
- alpha_offsets: int32 [36, 2], replicated, may hold values from 0 to 7
- alpha_mask: int32 [36, 2], replicated, may hold values 0 or 1
- beta_blocks: bfloat16 [48, 2, 128, 128], replicated, may hold values from -0.21875 to 0.21875
- beta_classes: int32 [8], replicated, may hold values from 1 to 10, 48 in all
- beta_offsets: int32 [48, 2], replicated, may hold values from 0 to 9
- beta_mask: int32 [48, 2], replicated, may hold values 0 or 1
Outputs:
- next_vector: float32 [4608, 6144], P('aa', 'ba')
- after_vector: float32 [4608, 6144], P('aa', 'ba')
The draws below stay inside these ranges and needn't reach their ends.
Inputs may be any that keep to these rules, and one draw needn't show every extreme that they name: `alpha_classes`: alpha strings are ordered by class; the class sizes sum to 36 blocks and one class has exactly 8 blocks. `beta_classes`: beta strings are ordered by class; the class sizes sum to 48 blocks and one class has exactly 10 blocks.
All inputs are finite; a program needn't handle non-finite values.
Results may differ from the reference program's by a relative error of at most 0.0065.
Values may be sent and summed in bfloat16 or wider, within the bound.
A program may use at most 64 MiB of HBM per device.

```python
import math
import jax
import jax.numpy as jnp
import numpy as np
from jax import lax

NA = 4608
NB = 6144
BLK = 128
NCLS = 8
A_MOST = 8
B_MOST = 10
SLOTS = 2
STEPS = 2
NBLK_A = 36
NBLK_B = 48


def place_ends(values, key, low, largest):
    spot = [jax.random.randint(jax.random.fold_in(key, axis), (), 0, length) for axis, length in enumerate(values.shape)]
    widest = values.shape.index(max(values.shape))
    neighbour = spot[:widest] + [(spot[widest] + 1) % values.shape[widest]] + spot[widest + 1:]
    return values.at[tuple(spot)].set(low).at[tuple(neighbour)].set(largest)


def level_of(own_key, extent, split, low, top_value):
    def one(axis_at, parts):
        draws = jax.random.uniform(jax.random.fold_in(jax.random.fold_in(own_key, 6), axis_at), (parts,), jnp.float32, low / len(split), top_value / len(split))
        return jnp.repeat(jnp.exp(draws), extent[axis_at] // parts).reshape((-1,) + (1,) * (len(extent) - axis_at - 1))

    level = one(*split[0])
    for cut in split[1:]:
        level = level * one(*cut)
    return level


def length_profile(count, total, bound, skew):
    weights = [(1 << 20) // math.isqrt(rank ** skew) + 1 for rank in range(2, count + 1)]
    spare, given = total - bound - (count - 1), [1] * (count - 1)
    while spare > 0:
        free = [i for i in range(count - 1) if given[i] < bound]
        whole, remaining = sum([weights[i] for i in free]), spare
        for i in free:
            more = min(bound - given[i], max(1, remaining * weights[i] // whole), spare)
            given[i] = given[i] + more
            spare = spare - more
    return np.array([bound] + given)


def uneven_parts(own_key, count, total, reach, slope):
    if count == 2:
        one = jax.random.randint(own_key, (), max(1, total - reach), min(reach, total - 1) + 1)
        return jnp.stack([one, total - one])
    lengths = jnp.asarray(length_profile(count, total, reach, slope), jnp.int32)
    twos = (count - 1) // 2
    source_of, taker = lengths[1:1 + 2 * twos:2], lengths[2:2 + 2 * twos:2]
    slack = jnp.minimum(source_of - 1, reach - taker)
    moved = jax.random.randint(jax.random.fold_in(own_key, 1), (twos,), 0, 1 << 20) % (slack + 1)
    lengths = lengths.at[1:1 + 2 * twos:2].set(source_of - moved).at[2:2 + 2 * twos:2].set(taker + moved)
    return lengths[jax.random.permutation(jax.random.fold_in(own_key, 2), count)]


def scatter_about(key, extent, deviation, most, split=(), held_as=jnp.bfloat16):
    drawn = deviation * jax.random.normal(key, extent, jnp.float32)
    if split:
        drawn = drawn * level_of(key, extent, split, -0.22, 0.18)
    return jnp.clip(drawn, -most, most).astype(held_as)


def setup_inputs(seed: int = 0) -> dict:
    streams_of = jax.random.split(jax.random.key(seed), 12)
    prev_vector = scatter_about(streams_of[0], (NA, NB), 1.0, 6.0, ((0, 96), (1, 8)), jnp.float32)
    this_vector = scatter_about(streams_of[1], (NA, NB), 1.0, 6.0, ((0, 96), (1, 8)), jnp.float32)
    diagonal = jnp.clip(jax.random.uniform(streams_of[2], (NA, NB), jnp.float32, -0.5, 0.5) * level_of(streams_of[2], (NA, NB), ((0, 96), (1, 8)), -0.4, 0.0), -0.5, 0.5)
    alpha_blocks = scatter_about(streams_of[3], (NBLK_A, SLOTS, BLK, BLK), (3 * SLOTS * BLK) ** -0.5, 0.21875)
    alpha_classes = uneven_parts(streams_of[4], NCLS, NBLK_A, A_MOST, 1).astype(jnp.int32)
    alpha_offsets = place_ends(jax.random.randint(streams_of[5], (NBLK_A, SLOTS), 0, A_MOST), jax.random.fold_in(streams_of[5], 1), 0, A_MOST - 1).astype(jnp.int32)
    alpha_mask = place_ends((jax.random.randint(streams_of[6], (NBLK_A, SLOTS), 0, 4) < 3).astype(jnp.int32), jax.random.fold_in(streams_of[6], 1), 0, 1)
    beta_blocks = scatter_about(streams_of[7], (NBLK_B, SLOTS, BLK, BLK), (3 * SLOTS * BLK) ** -0.5, 0.21875)
    beta_classes = uneven_parts(streams_of[8], NCLS, NBLK_B, B_MOST, 1).astype(jnp.int32)
    beta_offsets = place_ends(jax.random.randint(streams_of[9], (NBLK_B, SLOTS), 0, B_MOST), jax.random.fold_in(streams_of[9], 1), 0, B_MOST - 1).astype(jnp.int32)
    beta_mask = place_ends((jax.random.randint(streams_of[10], (NBLK_B, SLOTS), 0, 4) < 3).astype(jnp.int32), jax.random.fold_in(streams_of[10], 1), 0, 1)
    return {"prev_vector": prev_vector, "this_vector": this_vector, "diagonal": diagonal, "alpha_blocks": alpha_blocks, "alpha_classes": alpha_classes, "alpha_offsets": alpha_offsets, "alpha_mask": alpha_mask, "beta_blocks": beta_blocks, "beta_classes": beta_classes, "beta_offsets": beta_offsets, "beta_mask": beta_mask}


def block_columns(class_sizes, offsets):
    class_ends = jnp.cumsum(class_sizes).astype(jnp.int32)
    class_starts = class_ends - class_sizes
    row_ids = jnp.arange(offsets.shape[0], dtype=jnp.int32)[:, None]
    inside = (row_ids >= class_starts[None, :]) & (row_ids < class_ends[None, :])
    first_block = jnp.sum(jnp.where(inside, class_starts[None, :], 0), axis=1).astype(jnp.int32)
    class_length = jnp.sum(jnp.where(inside, class_sizes[None, :], 0), axis=1).astype(jnp.int32)
    return (first_block[:, None] + offsets % class_length[:, None]).astype(jnp.int32)


def couple_first(values_in, blocks, columns, live_mask):
    block_count, slot_count, block_size, _ = blocks.shape
    width = values_in.shape[1]
    stacked = values_in.reshape(block_count, block_size, width)
    result = jnp.zeros((block_count, block_size, width), jnp.float32)
    for which_slot in range(slot_count):
        weights = blocks[:, which_slot].astype(jnp.float32) * live_mask[:, which_slot, None, None].astype(jnp.float32)
        picked = stacked[columns[:, which_slot]]
        result = result + jnp.einsum("rij,rjb->rib", weights, picked, precision=lax.Precision.HIGHEST)
    return result.reshape(block_count * block_size, width)


def reference(prev_vector, this_vector, diagonal, alpha_blocks, alpha_classes, alpha_offsets, alpha_mask, beta_blocks, beta_classes, beta_offsets, beta_mask):
    alpha_cols = block_columns(alpha_classes, alpha_offsets)
    beta_cols = block_columns(beta_classes, beta_offsets)
    previous = prev_vector
    current = this_vector
    produced = []
    for iteration in range(STEPS):
        rounded = current.astype(jnp.bfloat16).astype(jnp.float32)
        alpha_term = couple_first(rounded, alpha_blocks, alpha_cols, alpha_mask).astype(jnp.bfloat16)
        beta_term = couple_first(rounded.T, beta_blocks, beta_cols, beta_mask).T.astype(jnp.bfloat16)
        newer = 2.0 * (alpha_term.astype(jnp.float32) + beta_term.astype(jnp.float32) + diagonal * current) - previous
        previous = current
        current = newer
        produced.append(newer)
    return produced[0], produced[-1]
```

```python
import jax
import jax.numpy as jnp
from jax import lax
from jax.experimental import pallas as pl
from jax.experimental.pallas import tpu as pltpu
from jax.sharding import PartitionSpec as P

BLK = 128
PLANES = 12
PLANE = 8
LINE = 8
ROWS = 48
COLB = 6
ROWB = 3
WIN = 10
TILE = 16
TILES = 3
PIECES = 27
YWIN = 24
NCLS = 8
MESH = pl.DeviceIdType.MESH


def remote(src, dst, send, recv, to):
    return pltpu.make_async_remote_copy(
        src_ref=src, dst_ref=dst, send_sem=send, recv_sem=recv, device_id=to, device_id_type=MESH
    )


def await_bytes(ref, sem):
    pltpu.make_async_copy(ref, ref, sem).wait()


def class_table(sizes):
    starts, lengths, first = [], [], jnp.int32(0)
    for c in range(NCLS):
        starts.append(first)
        lengths.append(sizes[c])
        first = first + sizes[c]
    return starts, lengths


def class_of(block, table):
    starts, lengths = table
    start, length = starts[0], lengths[0]
    for c in range(1, NCLS):
        later = block >= starts[c]
        start = jnp.where(later, starts[c], start)
        length = jnp.where(later, lengths[c], length)
    return start, length


def column_of(start, length, offset, halvings):
    for k in reversed(range(halvings)):
        step = length * (1 << k)
        offset = jnp.where(offset >= step, offset - step, offset)
    return start + offset


def kernel(
    prev_hbm, this_hbm, diag_hbm, ablk_hbm, acls, aoff, amask, bblk_hbm, bcls, boff, bmask,
    next_hbm, after_hbm,
    xv, pv, dv, tv, nv, ov, yw0, yw1, tb, win0, wint, win1, al0, al1, rec0, rec1, araw, braw, aw, bw,
    load_sem, store_sem, in_send, in_recv, out_send, out_recv, y_sem, self_sem,
):
    aa = lax.axis_index("aa")
    y = lax.axis_index("ba")
    z = lax.div(aa, PLANE)
    p = lax.rem(aa, PLANE)
    plane = {d: lax.rem(z + d + PLANES, PLANES) for d in (-2, -1, 0, 1, 2)}
    first = {d: plane[d] * PLANE for d in plane}
    line = {d: lax.rem(y + d + LINE, LINE) for d in (-2, -1, 1, 2)}
    is_home = p < COLB
    reaches = p < ROWB

    def at(d, q):
        return {"aa": first[d] + q, "ba": y}

    def along(d):
        return {"aa": aa, "ba": line[d]}

    loads = [pltpu.make_async_copy(this_hbm, xv, load_sem.at[0])]
    loads[0].start()

    barrier = pltpu.get_barrier_semaphore()

    def greet(to):
        pl.semaphore_signal(barrier, inc=1, device_id=to, device_id_type=MESH)

    for d in (-2, -1, 1, 2):
        greet(along(d))
    for d in (-1, 1):
        for q in range(PLANE):
            greet(at(d, q))
    for q in range(1, PLANE):
        greet(at(0, lax.rem(p + q, PLANE)))

    @pl.when(reaches)
    def _():
        for q in range(COLB):
            greet(at(-2, q))

    @pl.when(is_home)
    def _():
        for q in range(ROWB):
            greet(at(2, q))

    loads += [
        pltpu.make_async_copy(diag_hbm, dv, load_sem.at[1]),
        pltpu.make_async_copy(prev_hbm, pv, load_sem.at[2]),
        pltpu.make_async_copy(bblk_hbm.at[pl.ds(y * COLB, COLB)], braw, load_sem.at[3]),
    ]
    for k, (d, count) in enumerate(((-1, ROWB), (0, ROWB), (1, ROWB), (2, 1))):
        loads.append(
            pltpu.make_async_copy(
                ablk_hbm.at[pl.ds(plane[d] * ROWB, count)],
                araw.at[pl.ds(ROWB * k, count)],
                load_sem.at[4 + k],
            )
        )
    for c in loads[1:]:
        c.start()

    loads[0].wait()
    for cb in range(COLB):
        yw0[9 + cb] = xv[:, cb * BLK : (cb + 1) * BLK].astype(jnp.bfloat16).reshape(TILES, TILE, BLK)

    pl.semaphore_wait(barrier, 27 + jnp.where(reaches, COLB, 0) + jnp.where(is_home, ROWB, 0))

    def y_copies(w, step):
        parts = ((9, 6, 3, 1), (9, 6, 15, -1), (12, 3, 0, 2), (9, 3, 21, -2))
        return [
            remote(
                w.at[pl.ds(src, n)], w.at[pl.ds(dst, n)],
                y_sem.at[step, 0, k], y_sem.at[step, 1, k], along(d),
            )
            for k, (src, n, dst, d) in enumerate(parts)
        ]

    def piece(k):
        return pl.ds(TILES * k, TILES)

    def send_in(src, w, step):
        @pl.when(reaches)
        def _():
            for cb in range(COLB):
                remote(
                    src(cb), w.at[piece(3 * PLANE + p)],
                    in_send.at[step, 0], in_recv.at[step], at(-2, cb),
                ).start()

        for d, base in ((-1, 2 * PLANE), (1, 0)):
            for cb in range(COLB):
                remote(
                    src(cb), w.at[piece(base + p)], in_send.at[step, 1], in_recv.at[step], at(d, cb)
                ).start()
        for cb in range(COLB):

            @pl.when(p != cb)
            def _(cb=cb):
                remote(
                    src(cb), w.at[piece(PLANE + p)],
                    in_send.at[step, 2], in_recv.at[step], at(0, cb),
                ).start()

            @pl.when(p == cb)
            def _(cb=cb):
                pltpu.make_async_copy(
                    src(cb), w.at[piece(PLANE + p)], self_sem.at[step]
                ).start()

    def sent_in(step):
        @pl.when(reaches)
        def _():
            await_bytes(win0.at[pl.ds(0, COLB * TILES)], in_send.at[step, 0])

        await_bytes(win0.at[pl.ds(0, 2 * COLB * TILES)], in_send.at[step, 1])

        @pl.when(is_home)
        def _():
            await_bytes(win0.at[pl.ds(0, (COLB - 1) * TILES)], in_send.at[step, 2])

        @pl.when(jnp.logical_not(is_home))
        def _():
            await_bytes(win0.at[pl.ds(0, COLB * TILES)], in_send.at[step, 2])

    def arrived_in(w, step):
        await_bytes(w.at[pl.ds(0, (PIECES - 1) * TILES)], in_recv.at[step])
        await_bytes(w.at[pl.ds(0, TILES)], self_sem.at[step])

    def send_out(src, rec, step):
        for q in range(ROWB):
            remote(
                src.at[piece(3 * PLANE + q)], rec.at[3, p],
                out_send.at[step], out_recv.at[step, 1], at(2, q),
            ).start()
        for d, base, slot in ((1, 2 * PLANE, 0), (-1, 0, 2)):
            for q in range(PLANE):
                remote(
                    src.at[piece(base + q)], rec.at[slot, p],
                    out_send.at[step], out_recv.at[step, 0], at(d, q),
                ).start()
        for k in range(1, PLANE):
            q = lax.rem(p + k, PLANE)
            remote(
                src.at[piece(PLANE + q)], rec.at[1, p],
                out_send.at[step], out_recv.at[step, 0], at(0, q),
            ).start()
        pltpu.make_async_copy(
            src.at[piece(PLANE + p)], rec.at[1, p], self_sem.at[2 + step]
        ).start()

    def arrived_out(rec, step):
        @pl.when(reaches)
        def _():
            await_bytes(rec.at[3], out_recv.at[step, 1])

        @pl.when(is_home)
        def _():
            await_bytes(win0.at[pl.ds(0, (3 * COLB - 1) * TILES)], out_recv.at[step, 0])
            await_bytes(rec.at[3, 0], self_sem.at[2 + step])

        @pl.when(jnp.logical_not(is_home))
        def _():
            await_bytes(win0.at[pl.ds(0, 3 * COLB * TILES)], out_recv.at[step, 0])

    ys0 = y_copies(yw0, 0)
    for c in ys0:
        c.start()
    send_in(lambda cb: yw0.at[9 + cb], win0, 0)

    a_table = class_table(acls)
    b_table = class_table(bcls)
    a_at = []
    for j in range(WIN):
        block = lax.rem(z * ROWB - ROWB + j + PLANES * ROWB, PLANES * ROWB)
        start, length = class_of(block, a_table)
        a_at.append(
            [
                jnp.clip(
                    column_of(start, length, aoff[k, block], 3) - (z - 1) * ROWB, 0, WIN - 1
                )
                for k in range(2)
            ]
        )
    b_at = []
    for r in range(COLB):
        block = y * COLB + r
        start, length = class_of(block, b_table)
        b_at.append(
            [
                jnp.clip(
                    column_of(start, length, boff[k, block], 4) - y * COLB + 9, 0, YWIN - 1
                )
                for k in range(2)
            ]
        )
    slot_at = []
    for q in range(3):
        start, length = class_of(z * ROWB + lax.div(3 * p + q, PLANE), a_table)
        middle = start + lax.div(length - 1, 2)
        away = lax.div(middle, ROWB) - z
        slot_at.append(jnp.clip(jnp.where(away == -2, 3, away + 1), 0, 3))

    for c in loads[1:]:
        c.wait()
    for r in range(COLB):
        for k in range(2):
            live = bmask[k, y * COLB + r].astype(jnp.float32)
            bw[r, :, k * BLK : (k + 1) * BLK] = (braw[r, k].astype(jnp.float32) * live).astype(
                jnp.bfloat16
            )

    @pl.when(is_home)
    def _():
        for j in range(WIN):
            block = lax.rem(z * ROWB - ROWB + j + PLANES * ROWB, PLANES * ROWB)
            for k in range(2):
                live = amask[k, block].astype(jnp.float32)
                aw[j, :, k * BLK : (k + 1) * BLK] = (
                    araw[j, k].astype(jnp.float32) * live
                ).astype(jnp.bfloat16)
        al0[8 * WIN] = jnp.zeros((TILE, BLK), jnp.bfloat16)
        al1[8 * WIN] = jnp.zeros((TILE, BLK), jnp.bfloat16)

    def beta(w, r):
        both = jnp.concatenate([w[b_at[r][k]].reshape(ROWS, BLK) for k in range(2)], axis=1)
        out = lax.dot_general(
            both, bw[r], (((1,), (1,)), ((), ())), preferred_element_type=jnp.float32
        )
        return out.astype(jnp.bfloat16).astype(jnp.float32)

    def alpha(w, out):
        for j in range(WIN):
            both = jnp.concatenate(
                [w[pl.ds(a_at[j][k] * 8, 8)].reshape(BLK, BLK) for k in range(2)], axis=0
            )
            product = jnp.dot(aw[j], both, preferred_element_type=jnp.float32)
            out[8 * j : 8 * (j + 1)] = product.astype(jnp.bfloat16).reshape(8, TILE, BLK)

    def returned(rec, cb):
        return jnp.concatenate(
            [rec[slot_at[q], cb, q] for q in range(TILES)], axis=0
        ).astype(jnp.float32)

    for c in ys0:
        c.wait_recv()
    for cb in range(COLB):
        cols = slice(cb * BLK, (cb + 1) * BLK)
        t = 2.0 * (beta(yw0, cb) + dv[:, cols] * xv[:, cols]) - pv[:, cols]
        tv[:, cols] = t
        tb[cb] = t.astype(jnp.bfloat16).reshape(TILES, TILE, BLK)
    send_in(lambda cb: tb.at[cb], wint, 1)

    @pl.when(is_home)
    def _():
        arrived_in(win0, 0)
        alpha(win0, al0)
        send_out(al0, rec0, 0)
        arrived_in(wint, 1)
        for j in range(WIN):
            rows = slice(8 * j, 8 * (j + 1))
            win1[rows] = (
                2.0 * al0[rows].astype(jnp.float32) + wint[rows].astype(jnp.float32)
            ).astype(jnp.bfloat16)
        alpha(win1, al1)
        send_out(al1, rec1, 1)

    arrived_out(rec0, 0)
    for cb in range(COLB):
        cols = slice(cb * BLK, (cb + 1) * BLK)
        x1 = 2.0 * returned(rec0, cb) + tv[:, cols]
        nv[:, cols] = x1
        yw1[9 + cb] = x1.astype(jnp.bfloat16).reshape(TILES, TILE, BLK)
    ys1 = y_copies(yw1, 1)
    for c in ys1:
        c.start()
    stored = pltpu.make_async_copy(nv, next_hbm, store_sem.at[0])
    stored.start()
    for cb in range(COLB):
        cols = slice(cb * BLK, (cb + 1) * BLK)
        tv[:, cols] = 2.0 * (dv[:, cols] * nv[:, cols]) - xv[:, cols]
    for c in ys1:
        c.wait_recv()
    for cb in range(COLB):
        cols = slice(cb * BLK, (cb + 1) * BLK)
        tv[:, cols] = tv[:, cols] + 2.0 * beta(yw1, cb)
    arrived_out(rec1, 1)
    for cb in range(COLB):
        cols = slice(cb * BLK, (cb + 1) * BLK)
        ov[:, cols] = tv[:, cols] + 2.0 * returned(rec1, cb)
    last = pltpu.make_async_copy(ov, after_hbm, store_sem.at[1])
    last.start()

    for step in range(2):
        sent_in(step)

        @pl.when(is_home)
        def _(step=step):
            await_bytes(win0.at[pl.ds(0, (PIECES - 1) * TILES)], out_send.at[step])

    for c in ys0 + ys1:
        c.wait_send()
    stored.wait()
    last.wait()


def on_device(prev, this, diag, ablk, acls, aoff, amask, bblk, bcls, boff, bmask):
    rows, columns = ROWS, COLB * BLK
    f32, bf16 = jnp.float32, jnp.bfloat16
    hbm = pl.BlockSpec(memory_space=pltpu.HBM)
    smem = pl.BlockSpec(memory_space=pltpu.SMEM)
    dma = pltpu.SemaphoreType.DMA
    next_vector, after_vector = pl.pallas_call(
        kernel,
        out_shape=[jax.ShapeDtypeStruct((rows, columns), f32)] * 2,
        in_specs=[hbm, hbm, hbm, hbm, smem, smem, smem, hbm, smem, smem, smem],
        out_specs=[hbm, hbm],
        scratch_shapes=[
            *[pltpu.VMEM((rows, columns), f32)] * 6,
            *[pltpu.VMEM((YWIN, TILES, TILE, BLK), bf16)] * 2,
            pltpu.VMEM((COLB, TILES, TILE, BLK), bf16),
            *[pltpu.VMEM((PIECES * TILES, TILE, BLK), bf16)] * 5,
            *[pltpu.VMEM((4, COLB, TILES, TILE, BLK), bf16)] * 2,
            pltpu.VMEM((WIN, 2, BLK, BLK), bf16),
            pltpu.VMEM((COLB, 2, BLK, BLK), bf16),
            pltpu.VMEM((WIN, BLK, 2 * BLK), bf16),
            pltpu.VMEM((COLB, BLK, 2 * BLK), bf16),
            dma((8,)),
            dma((2,)),
            dma((2, 3)),
            dma((2,)),
            dma((2,)),
            dma((2, 2)),
            dma((2, 2, 4)),
            dma((4,)),
        ],
        compiler_params=pltpu.CompilerParams(
            collective_id=0, has_side_effects=True, vmem_limit_bytes=60 * 1024 * 1024
        ),
        name="chebyshev_steps",
    )(prev, this, diag, ablk, acls, aoff.T, amask.T, bblk, bcls, boff.T, bmask.T)
    return next_vector, after_vector


def solution(mesh):
    own = P("aa", "ba")
    return jax.shard_map(
        on_device,
        mesh=mesh,
        in_specs=(own, own, own, *[P()] * 8),
        out_specs=(own, own),
        check_vma=False,
    )
```

```python
import jax
import jax.numpy as jnp
from jax import lax
from jax.experimental import pallas as pl
from jax.experimental.pallas import tpu as pltpu
from jax.sharding import PartitionSpec as P

BLK = 128
PLANES = 12
PLANE = 8
LINE = 8
ROWS = 48
COLB = 6
ROWB = 3
WIN = 10
TILE = 16
TILES = 3
PIECES = 27
YWIN = 24
NCLS = 8
MESH = pl.DeviceIdType.MESH


def remote(src, dst, send, recv, to):
    return pltpu.make_async_remote_copy(
        src_ref=src, dst_ref=dst, send_sem=send, recv_sem=recv, device_id=to, device_id_type=MESH
    )


def await_bytes(ref, sem):
    pltpu.make_async_copy(ref, ref, sem).wait()


def class_table(sizes):
    starts, lengths, first = [], [], jnp.int32(0)
    for c in range(NCLS):
        starts.append(first)
        lengths.append(sizes[c])
        first = first + sizes[c]
    return starts, lengths


def class_of(block, table):
    starts, lengths = table
    start, length = starts[0], lengths[0]
    for c in range(1, NCLS):
        later = block >= starts[c]
        start = jnp.where(later, starts[c], start)
        length = jnp.where(later, lengths[c], length)
    return start, length


def column_of(start, length, offset, halvings):
    for k in reversed(range(halvings)):
        step = length * (1 << k)
        offset = jnp.where(offset >= step, offset - step, offset)
    return start + offset


def kernel(
    prev_hbm, this_hbm, diag_hbm, ablk_hbm, acls, aoff, amask, bblk_hbm, bcls, boff, bmask,
    next_hbm, after_hbm,
    xv, pv, dv, tv, nv, ov, yw0, yw1, tb, win0, wint, win1, al0, al1, rec0, rec1, araw, braw, aw, bw,
    load_sem, store_sem, in_send, in_recv, out_send, out_recv, y_sem, self_sem,
):
    aa = lax.axis_index("aa")
    y = lax.axis_index("ba")
    z = lax.div(aa, PLANE)
    p = lax.rem(aa, PLANE)
    plane = {d: lax.rem(z + d + PLANES, PLANES) for d in (-2, -1, 0, 1, 2)}
    first = {d: plane[d] * PLANE for d in plane}
    line = {d: lax.rem(y + d + LINE, LINE) for d in (-2, -1, 1, 2)}
    is_home = p < COLB
    reaches = p < ROWB

    def at(d, q):
        return {"aa": first[d] + q, "ba": y}

    def along(d):
        return {"aa": aa, "ba": line[d]}

    loads = [pltpu.make_async_copy(this_hbm, xv, load_sem.at[0])]
    loads[0].start()

    barrier = pltpu.get_barrier_semaphore()

    def greet(to):
        pl.semaphore_signal(barrier, inc=1, device_id=to, device_id_type=MESH)

    for d in (-2, -1, 1, 2):
        greet(along(d))
    for d in (-1, 1):
        for q in range(PLANE):
            greet(at(d, q))
    for q in range(1, PLANE):
        greet(at(0, lax.rem(p + q, PLANE)))

    @pl.when(reaches)
    def _():
        for q in range(COLB):
            greet(at(-2, q))

    @pl.when(is_home)
    def _():
        for q in range(ROWB):
            greet(at(2, q))

    loads += [
        pltpu.make_async_copy(diag_hbm, dv, load_sem.at[1]),
        pltpu.make_async_copy(prev_hbm, pv, load_sem.at[2]),
        pltpu.make_async_copy(bblk_hbm.at[pl.ds(y * COLB, COLB)], braw, load_sem.at[3]),
    ]
    for k, (d, count) in enumerate(((-1, ROWB), (0, ROWB), (1, ROWB), (2, 1))):
        loads.append(
            pltpu.make_async_copy(
                ablk_hbm.at[pl.ds(plane[d] * ROWB, count)],
                araw.at[pl.ds(ROWB * k, count)],
                load_sem.at[4 + k],
            )
        )
    for c in loads[1:]:
        c.start()

    loads[0].wait()
    for cb in range(COLB):
        yw0[9 + cb] = xv[:, cb * BLK : (cb + 1) * BLK].astype(jnp.bfloat16).reshape(TILES, TILE, BLK)

    pl.semaphore_wait(barrier, 27 + jnp.where(reaches, COLB, 0) + jnp.where(is_home, ROWB, 0))

    def y_copies(w, step):
        parts = ((9, 6, 3, 1), (9, 6, 15, -1), (12, 3, 0, 2), (9, 3, 21, -2))
        return [
            remote(
                w.at[pl.ds(src, n)], w.at[pl.ds(dst, n)],
                y_sem.at[step, 0, k], y_sem.at[step, 1, k], along(d),
            )
            for k, (src, n, dst, d) in enumerate(parts)
        ]

    def piece(k):
        return pl.ds(TILES * k, TILES)

    def send_in(src, w, step, cb):
        @pl.when(reaches)
        def _():
            remote(
                src, w.at[piece(3 * PLANE + p)],
                in_send.at[step, 0], in_recv.at[step], at(-2, cb),
            ).start()

        for d, base in ((-1, 2 * PLANE), (1, 0)):
            remote(
                src, w.at[piece(base + p)], in_send.at[step, 1], in_recv.at[step], at(d, cb)
            ).start()

        @pl.when(p != cb)
        def _():
            remote(
                src, w.at[piece(PLANE + p)], in_send.at[step, 2], in_recv.at[step], at(0, cb)
            ).start()

        @pl.when(p == cb)
        def _():
            pltpu.make_async_copy(src, w.at[piece(PLANE + p)], self_sem.at[step]).start()

    def sent_in(step):
        @pl.when(reaches)
        def _():
            await_bytes(win0.at[pl.ds(0, COLB * TILES)], in_send.at[step, 0])

        await_bytes(win0.at[pl.ds(0, 2 * COLB * TILES)], in_send.at[step, 1])

        @pl.when(is_home)
        def _():
            await_bytes(win0.at[pl.ds(0, (COLB - 1) * TILES)], in_send.at[step, 2])

        @pl.when(jnp.logical_not(is_home))
        def _():
            await_bytes(win0.at[pl.ds(0, COLB * TILES)], in_send.at[step, 2])

    def arrived_in(w, step):
        await_bytes(w.at[pl.ds(0, (PIECES - 1) * TILES)], in_recv.at[step])
        await_bytes(w.at[pl.ds(0, TILES)], self_sem.at[step])

    def send_far(src, rec, step):
        for q in range(ROWB):
            remote(
                src.at[piece(3 * PLANE + q)], rec.at[3, p],
                out_send.at[step], out_recv.at[step, 1], at(2, q),
            ).start()

    def send_near(src, rec, step, d, base, slot):
        for q in range(PLANE):
            remote(
                src.at[piece(base + q)], rec.at[slot, p],
                out_send.at[step], out_recv.at[step, 0], at(d, q),
            ).start()

    def send_own(src, rec, step):
        for k in range(1, PLANE):
            q = lax.rem(p + k, PLANE)
            remote(
                src.at[piece(PLANE + q)], rec.at[1, p],
                out_send.at[step], out_recv.at[step, 0], at(0, q),
            ).start()
        pltpu.make_async_copy(
            src.at[piece(PLANE + p)], rec.at[1, p], self_sem.at[2 + step]
        ).start()

    def arrived_out(rec, step):
        @pl.when(reaches)
        def _():
            await_bytes(rec.at[3], out_recv.at[step, 1])

        @pl.when(is_home)
        def _():
            await_bytes(win0.at[pl.ds(0, (3 * COLB - 1) * TILES)], out_recv.at[step, 0])
            await_bytes(rec.at[3, 0], self_sem.at[2 + step])

        @pl.when(jnp.logical_not(is_home))
        def _():
            await_bytes(win0.at[pl.ds(0, 3 * COLB * TILES)], out_recv.at[step, 0])

    ys0 = y_copies(yw0, 0)
    for c in ys0:
        c.start()
    for cb in range(COLB):
        send_in(yw0.at[9 + cb], win0, 0, cb)

    a_table = class_table(acls)
    b_table = class_table(bcls)
    a_at = []
    for j in range(WIN):
        block = lax.rem(z * ROWB - ROWB + j + PLANES * ROWB, PLANES * ROWB)
        start, length = class_of(block, a_table)
        a_at.append(
            [
                jnp.clip(
                    column_of(start, length, aoff[k, block], 3) - (z - 1) * ROWB, 0, WIN - 1
                )
                for k in range(2)
            ]
        )
    b_at = []
    for r in range(COLB):
        block = y * COLB + r
        start, length = class_of(block, b_table)
        b_at.append(
            [
                jnp.clip(
                    column_of(start, length, boff[k, block], 4) - y * COLB + 9, 0, YWIN - 1
                )
                for k in range(2)
            ]
        )
    slot_at = []
    for q in range(3):
        start, length = class_of(z * ROWB + lax.div(3 * p + q, PLANE), a_table)
        middle = start + lax.div(length - 1, 2)
        away = lax.div(middle, ROWB) - z
        slot_at.append(jnp.clip(jnp.where(away == -2, 3, away + 1), 0, 3))

    for c in loads[1:]:
        c.wait()
    for r in range(COLB):
        for k in range(2):
            live = bmask[k, y * COLB + r].astype(jnp.float32)
            bw[r, :, k * BLK : (k + 1) * BLK] = (braw[r, k].astype(jnp.float32) * live).astype(
                jnp.bfloat16
            )

    @pl.when(is_home)
    def _():
        for j in range(WIN):
            block = lax.rem(z * ROWB - ROWB + j + PLANES * ROWB, PLANES * ROWB)
            for k in range(2):
                live = amask[k, block].astype(jnp.float32)
                aw[j, :, k * BLK : (k + 1) * BLK] = (
                    araw[j, k].astype(jnp.float32) * live
                ).astype(jnp.bfloat16)
        al0[8 * WIN] = jnp.zeros((TILE, BLK), jnp.bfloat16)
        al1[8 * WIN] = jnp.zeros((TILE, BLK), jnp.bfloat16)

    def beta(w, r):
        both = jnp.concatenate([w[b_at[r][k]].reshape(ROWS, BLK) for k in range(2)], axis=1)
        return lax.dot_general(
            both, bw[r], (((1,), (1,)), ((), ())), preferred_element_type=jnp.float32
        )

    def alpha(w, out, rows):
        for j in rows:
            both = jnp.concatenate(
                [w[pl.ds(a_at[j][k] * 8, 8)].reshape(BLK, BLK) for k in range(2)], axis=0
            )
            product = jnp.dot(aw[j], both, preferred_element_type=jnp.float32)
            out[8 * j : 8 * (j + 1)] = product.astype(jnp.bfloat16).reshape(8, TILE, BLK)

    def alpha_and_send(w, out, rec, step):
        alpha(w, out, range(9, 10))
        send_far(out, rec, step)
        alpha(w, out, range(6, 9))
        send_near(out, rec, step, 1, 2 * PLANE, 0)
        alpha(w, out, range(0, 3))
        send_near(out, rec, step, -1, 0, 2)
        alpha(w, out, range(3, 6))
        send_own(out, rec, step)

    def returned(rec, cb):
        return jnp.concatenate(
            [rec[slot_at[q], cb, q] for q in range(TILES)], axis=0
        ).astype(jnp.float32)

    for c in ys0:
        c.wait_recv()
    for cb in range(COLB):
        cols = slice(cb * BLK, (cb + 1) * BLK)
        b1 = beta(yw0, cb).astype(jnp.bfloat16).astype(jnp.float32)
        t = 2.0 * (b1 + dv[:, cols] * xv[:, cols]) - pv[:, cols]
        tv[:, cols] = t
        yw1[9 + cb] = t.astype(jnp.bfloat16).reshape(TILES, TILE, BLK)
        tb[cb] = (t + 2.0 * b1).astype(jnp.bfloat16).reshape(TILES, TILE, BLK)
        send_in(tb.at[cb], wint, 1, cb)
    ys1 = y_copies(yw1, 1)
    for c in ys1:
        c.start()

    @pl.when(is_home)
    def _():
        arrived_in(win0, 0)
        alpha_and_send(win0, al0, rec0, 0)
        arrived_in(wint, 1)
        for j in range(WIN):
            rows = slice(8 * j, 8 * (j + 1))
            win1[rows] = (
                2.0 * al0[rows].astype(jnp.float32) + wint[rows].astype(jnp.float32)
            ).astype(jnp.bfloat16)
        alpha_and_send(win1, al1, rec1, 1)

    arrived_out(rec0, 0)
    for cb in range(COLB):
        cols = slice(cb * BLK, (cb + 1) * BLK)
        nv[:, cols] = 2.0 * returned(rec0, cb) + tv[:, cols]
    stored = pltpu.make_async_copy(nv, next_hbm, store_sem.at[0])
    stored.start()
    for c in ys1:
        c.wait_recv()
    for cb in range(COLB):
        cols = slice(cb * BLK, (cb + 1) * BLK)
        tv[:, cols] = 2.0 * (beta(yw1, cb) + dv[:, cols] * nv[:, cols]) - xv[:, cols]
    arrived_out(rec1, 1)
    for cb in range(COLB):
        cols = slice(cb * BLK, (cb + 1) * BLK)
        ov[:, cols] = tv[:, cols] + 2.0 * returned(rec1, cb)
    last = pltpu.make_async_copy(ov, after_hbm, store_sem.at[1])
    last.start()

    for step in range(2):
        sent_in(step)

        @pl.when(is_home)
        def _(step=step):
            await_bytes(win0.at[pl.ds(0, (PIECES - 1) * TILES)], out_send.at[step])

    for c in ys0 + ys1:
        c.wait_send()
    stored.wait()
    last.wait()


def hand_over(next_in, after_in, next_out, after_out, held, sem):
    pairs = ((next_in, next_out), (after_in, after_out))
    taken = [pltpu.make_async_copy(c[0], held.at[k], sem.at[0, k]) for k, c in enumerate(pairs)]
    given = [pltpu.make_async_copy(held.at[k], c[1], sem.at[1, k]) for k, c in enumerate(pairs)]
    for c in taken:
        c.start()
    for k in range(2):
        taken[k].wait()
        given[k].start()
    for c in given:
        c.wait()


def on_device(prev, this, diag, ablk, acls, aoff, amask, bblk, bcls, boff, bmask):
    rows, columns = ROWS, COLB * BLK
    f32, bf16 = jnp.float32, jnp.bfloat16
    hbm = pl.BlockSpec(memory_space=pltpu.HBM)
    smem = pl.BlockSpec(memory_space=pltpu.SMEM)
    dma = pltpu.SemaphoreType.DMA
    next_vector, after_vector = pl.pallas_call(
        kernel,
        out_shape=[jax.ShapeDtypeStruct((rows, columns), f32)] * 2,
        in_specs=[hbm, hbm, hbm, hbm, smem, smem, smem, hbm, smem, smem, smem],
        out_specs=[hbm, hbm],
        scratch_shapes=[
            *[pltpu.VMEM((rows, columns), f32)] * 6,
            *[pltpu.VMEM((YWIN, TILES, TILE, BLK), bf16)] * 2,
            pltpu.VMEM((COLB, TILES, TILE, BLK), bf16),
            *[pltpu.VMEM((PIECES * TILES, TILE, BLK), bf16)] * 5,
            *[pltpu.VMEM((4, COLB, TILES, TILE, BLK), bf16)] * 2,
            pltpu.VMEM((WIN, 2, BLK, BLK), bf16),
            pltpu.VMEM((COLB, 2, BLK, BLK), bf16),
            pltpu.VMEM((WIN, BLK, 2 * BLK), bf16),
            pltpu.VMEM((COLB, BLK, 2 * BLK), bf16),
            dma((8,)),
            dma((2,)),
            dma((2, 3)),
            dma((2,)),
            dma((2,)),
            dma((2, 2)),
            dma((2, 2, 4)),
            dma((4,)),
        ],
        compiler_params=pltpu.CompilerParams(
            collective_id=0, has_side_effects=True, vmem_limit_bytes=60 * 1024 * 1024
        ),
        name="chebyshev_steps",
    )(prev, this, diag, ablk, acls, aoff.T, amask.T, bblk, bcls, boff.T, bmask.T)
    return pl.pallas_call(
        hand_over,
        out_shape=[jax.ShapeDtypeStruct((rows, columns), f32)] * 2,
        in_specs=[hbm, hbm],
        out_specs=[hbm, hbm],
        scratch_shapes=[pltpu.VMEM((2, rows, columns), f32), dma((2, 2))],
        compiler_params=pltpu.CompilerParams(vmem_limit_bytes=60 * 1024 * 1024),
        name="hand_over",
    )(next_vector, after_vector)


def solution(mesh):
    own = P("aa", "ba")
    return jax.shard_map(
        on_device,
        mesh=mesh,
        in_specs=(own, own, own, *[P()] * 8),
        out_specs=(own, own),
        check_vma=False,
    )
```

```python
import jax
import jax.numpy as jnp
from jax import lax
from jax.experimental import pallas as pl
from jax.experimental.pallas import tpu as pltpu
from jax.sharding import PartitionSpec as P

BLK = 128
PLANES = 12
PLANE = 8
LINE = 8
ROWS = 48
COLB = 6
HOME = 2
ROWB = 3
WIN = 10
TILE = 16
TILES = 3
PIECES = 27
YWIN = 24
NCLS = 8
MESH = pl.DeviceIdType.MESH


def remote(src, dst, send, recv, to):
    return pltpu.make_async_remote_copy(
        src_ref=src, dst_ref=dst, send_sem=send, recv_sem=recv, device_id=to, device_id_type=MESH
    )


def await_bytes(ref, sem):
    pltpu.make_async_copy(ref, ref, sem).wait()


def class_table(sizes):
    starts, lengths, first = [], [], jnp.int32(0)
    for c in range(NCLS):
        starts.append(first)
        lengths.append(sizes[c])
        first = first + sizes[c]
    return starts, lengths


def class_of(block, table):
    starts, lengths = table
    start, length = starts[0], lengths[0]
    for c in range(1, NCLS):
        later = block >= starts[c]
        start = jnp.where(later, starts[c], start)
        length = jnp.where(later, lengths[c], length)
    return start, length


def column_of(start, length, offset, halvings):
    for k in reversed(range(halvings)):
        step = length * (1 << k)
        offset = jnp.where(offset >= step, offset - step, offset)
    return start + offset


def kernel(
    prev_hbm, this_hbm, diag_hbm, ablk_hbm, acls, aoff, amask, bblk_hbm, bcls, boff, bmask,
    next_hbm, after_hbm,
    xv, pv, dv, tv, nv, ov, yw0, yw1, tb, win0, wint, win1, al0, al1, rec0, rec1, araw, braw, aw, bw,
    load_sem, store_sem, in_send, in_recv, out_send, out_recv, y_sem, self_sem,
):
    aa = lax.axis_index("aa")
    y = lax.axis_index("ba")
    z = lax.div(aa, PLANE)
    p = lax.rem(aa, PLANE)
    is_home = p >= HOME
    reaches = p < ROWB
    has_plane = {d: (z >= -d) if d < 0 else (z < PLANES - d) for d in (-2, -1, 1, 2)}
    has_line = {d: (y >= -d) if d < 0 else (y < LINE - d) for d in (-2, -1, 1, 2)}
    sends_far = jnp.logical_and(reaches, has_plane[-2])
    homes_far = jnp.logical_and(is_home, has_plane[2])

    def at(d, q):
        return {"aa": aa + (d * PLANE - p) + q, "ba": y}

    def along(d):
        return {"aa": aa, "ba": y + d}

    loads = [pltpu.make_async_copy(this_hbm, xv, load_sem.at[0])]
    loads[0].start()

    barrier = pltpu.get_barrier_semaphore()

    def greet(to):
        pl.semaphore_signal(barrier, inc=1, device_id=to, device_id_type=MESH)

    for d in (-2, -1, 1, 2):

        @pl.when(has_line[d])
        def _(d=d):
            greet(along(d))

    for d in (-1, 1):

        @pl.when(has_plane[d])
        def _(d=d):
            for q in range(PLANE):
                greet(at(d, q))

    for q in range(1, PLANE):
        greet(at(0, lax.rem(p + q, PLANE)))

    @pl.when(sends_far)
    def _():
        for cb in range(COLB):
            greet(at(-2, HOME + cb))

    @pl.when(homes_far)
    def _():
        for q in range(ROWB):
            greet(at(2, q))

    loads += [
        pltpu.make_async_copy(diag_hbm, dv, load_sem.at[1]),
        pltpu.make_async_copy(prev_hbm, pv, load_sem.at[2]),
        pltpu.make_async_copy(bblk_hbm.at[pl.ds(y * COLB, COLB)], braw, load_sem.at[3]),
    ]
    for k, (d, count) in enumerate(((-1, ROWB), (0, ROWB), (1, ROWB), (2, 1))):
        held = lax.rem(z + d + PLANES, PLANES)
        loads.append(
            pltpu.make_async_copy(
                ablk_hbm.at[pl.ds(held * ROWB, count)],
                araw.at[pl.ds(ROWB * k, count)],
                load_sem.at[4 + k],
            )
        )
    for c in loads[1:]:
        c.start()

    loads[0].wait()
    for cb in range(COLB):
        yw0[9 + cb] = xv[:, cb * BLK : (cb + 1) * BLK].astype(jnp.bfloat16).reshape(TILES, TILE, BLK)

    greetings = PLANE - 1 + jnp.where(sends_far, COLB, 0) + jnp.where(homes_far, ROWB, 0)
    for d in (-2, -1, 1, 2):
        greetings = greetings + jnp.where(has_line[d], 1, 0)
    for d in (-1, 1):
        greetings = greetings + jnp.where(has_plane[d], PLANE, 0)
    pl.semaphore_wait(barrier, greetings)

    def y_copy(w, step, k):
        src, n, dst, d = ((9, 6, 3, 1), (9, 6, 15, -1), (12, 3, 0, 2), (9, 3, 21, -2))[k]
        return d, remote(
            w.at[pl.ds(src, n)], w.at[pl.ds(dst, n)],
            y_sem.at[step, 0, k], y_sem.at[step, 1, k], along(d),
        )

    def y_start(w, step):
        for k in range(4):
            d, copy = y_copy(w, step, k)
            pl.when(has_line[d])(copy.start)

    def y_sent(w, step):
        for k in range(4):
            d, copy = y_copy(w, step, k)
            pl.when(has_line[d])(copy.wait_send)

    def y_arrived(w, step):
        for k in range(4):
            d, copy = y_copy(w, step, k)
            pl.when(has_line[-d])(copy.wait_recv)

    def piece(k):
        return pl.ds(TILES * k, TILES)

    def send_in(src, w, step, cb):
        to = HOME + cb

        @pl.when(sends_far)
        def _():
            remote(
                src, w.at[piece(3 * PLANE + p)],
                in_send.at[step, 3], in_recv.at[step, 3], at(-2, to),
            ).start()

        for k, d, base in ((2, -1, 2 * PLANE), (0, 1, 0)):

            @pl.when(has_plane[d])
            def _(k=k, d=d, base=base):
                remote(
                    src, w.at[piece(base + p)],
                    in_send.at[step, k], in_recv.at[step, k], at(d, to),
                ).start()

        @pl.when(p != to)
        def _():
            remote(
                src, w.at[piece(PLANE + p)], in_send.at[step, 1], in_recv.at[step, 1], at(0, to)
            ).start()

        @pl.when(p == to)
        def _():
            pltpu.make_async_copy(src, w.at[piece(PLANE + p)], self_sem.at[step]).start()

    def await_pieces(count, sem):
        await_bytes(win0.at[pl.ds(0, count * TILES)], sem)

    def sent_in(step):
        pl.when(sends_far)(lambda: await_pieces(COLB, in_send.at[step, 3]))
        pl.when(has_plane[-1])(lambda: await_pieces(COLB, in_send.at[step, 2]))
        pl.when(has_plane[1])(lambda: await_pieces(COLB, in_send.at[step, 0]))
        pl.when(is_home)(lambda: await_pieces(COLB - 1, in_send.at[step, 1]))
        pl.when(jnp.logical_not(is_home))(lambda: await_pieces(COLB, in_send.at[step, 1]))

    def arrived_in(step):
        await_pieces(1, self_sem.at[step])
        await_pieces(PLANE - 1, in_recv.at[step, 1])
        pl.when(has_plane[-1])(lambda: await_pieces(PLANE, in_recv.at[step, 0]))
        pl.when(has_plane[1])(lambda: await_pieces(PLANE, in_recv.at[step, 2]))
        pl.when(has_plane[2])(lambda: await_pieces(ROWB, in_recv.at[step, 3]))

    def send_out(src, rec, step, d, base, slot, count):
        @pl.when(has_plane[d])
        def _():
            for q in range(count):
                remote(
                    src.at[piece(base + q)], rec.at[slot, p - HOME],
                    out_send.at[step, slot], out_recv.at[step, slot], at(d, q),
                ).start()

    def send_own(src, rec, step):
        for k in range(1, PLANE):
            q = lax.rem(p + k, PLANE)
            remote(
                src.at[piece(PLANE + q)], rec.at[1, p - HOME],
                out_send.at[step, 1], out_recv.at[step, 1], at(0, q),
            ).start()
        pltpu.make_async_copy(
            src.at[piece(PLANE + p)], rec.at[1, p - HOME], self_sem.at[2 + step]
        ).start()

    def sent_out(step):
        await_pieces(PLANE - 1, out_send.at[step, 1])
        pl.when(has_plane[2])(lambda: await_pieces(ROWB, out_send.at[step, 3]))
        pl.when(has_plane[1])(lambda: await_pieces(PLANE, out_send.at[step, 0]))
        pl.when(has_plane[-1])(lambda: await_pieces(PLANE, out_send.at[step, 2]))

    def arrived_out(step):
        pl.when(sends_far)(lambda: await_pieces(COLB, out_recv.at[step, 3]))
        pl.when(has_plane[-1])(lambda: await_pieces(COLB, out_recv.at[step, 0]))
        pl.when(has_plane[1])(lambda: await_pieces(COLB, out_recv.at[step, 2]))
        pl.when(jnp.logical_not(is_home))(lambda: await_pieces(COLB, out_recv.at[step, 1]))

        @pl.when(is_home)
        def _():
            await_pieces(COLB - 1, out_recv.at[step, 1])
            await_pieces(1, self_sem.at[2 + step])

    y_start(yw0, 0)
    for cb in range(COLB):
        send_in(yw0.at[9 + cb], win0, 0, cb)

    a_table = class_table(acls)
    b_table = class_table(bcls)
    a_at = []
    for j in range(WIN):
        block = lax.rem(z * ROWB - ROWB + j + PLANES * ROWB, PLANES * ROWB)
        start, length = class_of(block, a_table)
        a_at.append(
            [
                jnp.clip(
                    column_of(start, length, aoff[k, block], 3) - (z - 1) * ROWB, 0, WIN - 1
                )
                for k in range(2)
            ]
        )
    b_at = []
    for r in range(COLB):
        block = y * COLB + r
        start, length = class_of(block, b_table)
        b_at.append(
            [
                jnp.clip(
                    column_of(start, length, boff[k, block], 4) - y * COLB + 9, 0, YWIN - 1
                )
                for k in range(2)
            ]
        )
    slot_at = []
    for q in range(3):
        start, length = class_of(z * ROWB + lax.div(3 * p + q, PLANE), a_table)
        middle = start + lax.div(length - 1, 2)
        away = lax.div(middle, ROWB) - z
        slot_at.append(jnp.clip(jnp.where(away == -2, 3, away + 1), 0, 3))

    for c in loads[1:]:
        c.wait()
    for r in range(COLB):
        for k in range(2):
            live = bmask[k, y * COLB + r].astype(jnp.float32)
            bw[r, :, k * BLK : (k + 1) * BLK] = (braw[r, k].astype(jnp.float32) * live).astype(
                jnp.bfloat16
            )

    @pl.when(is_home)
    def _():
        for j in range(WIN):
            block = lax.rem(z * ROWB - ROWB + j + PLANES * ROWB, PLANES * ROWB)
            for k in range(2):
                live = amask[k, block].astype(jnp.float32)
                aw[j, :, k * BLK : (k + 1) * BLK] = (
                    araw[j, k].astype(jnp.float32) * live
                ).astype(jnp.bfloat16)
        al0[8 * WIN] = jnp.zeros((TILE, BLK), jnp.bfloat16)
        al1[8 * WIN] = jnp.zeros((TILE, BLK), jnp.bfloat16)

    def beta(w, r):
        both = jnp.concatenate([w[b_at[r][k]].reshape(ROWS, BLK) for k in range(2)], axis=1)
        return lax.dot_general(
            both, bw[r], (((1,), (1,)), ((), ())), preferred_element_type=jnp.float32
        )

    def alpha(w, out, rows):
        for j in rows:
            both = jnp.concatenate(
                [w[pl.ds(a_at[j][k] * 8, 8)].reshape(BLK, BLK) for k in range(2)], axis=0
            )
            product = jnp.dot(aw[j], both, preferred_element_type=jnp.float32)
            out[8 * j : 8 * (j + 1)] = product.astype(jnp.bfloat16).reshape(8, TILE, BLK)

    def alpha_and_send(w, out, rec, step):
        alpha(w, out, range(9, 10))
        send_out(out, rec, step, 2, 3 * PLANE, 3, ROWB)
        alpha(w, out, range(6, 9))
        send_out(out, rec, step, 1, 2 * PLANE, 0, PLANE)
        alpha(w, out, range(0, 3))
        send_out(out, rec, step, -1, 0, 2, PLANE)
        alpha(w, out, range(3, 6))
        send_own(out, rec, step)

    def returned(rec, cb):
        return jnp.concatenate(
            [rec[slot_at[q], cb, q] for q in range(TILES)], axis=0
        ).astype(jnp.float32)

    y_arrived(yw0, 0)
    for cb in range(COLB):
        cols = slice(cb * BLK, (cb + 1) * BLK)
        b1 = beta(yw0, cb).astype(jnp.bfloat16).astype(jnp.float32)
        t = 2.0 * (b1 + dv[:, cols] * xv[:, cols]) - pv[:, cols]
        tv[:, cols] = t
        yw1[9 + cb] = t.astype(jnp.bfloat16).reshape(TILES, TILE, BLK)
        tb[cb] = (t + 2.0 * b1).astype(jnp.bfloat16).reshape(TILES, TILE, BLK)
        send_in(tb.at[cb], wint, 1, cb)
    y_start(yw1, 1)

    @pl.when(is_home)
    def _():
        arrived_in(0)
        alpha_and_send(win0, al0, rec0, 0)
        arrived_in(1)
        for j in range(WIN):
            rows = slice(8 * j, 8 * (j + 1))
            win1[rows] = (
                2.0 * al0[rows].astype(jnp.float32) + wint[rows].astype(jnp.float32)
            ).astype(jnp.bfloat16)
        alpha_and_send(win1, al1, rec1, 1)

    arrived_out(0)
    for cb in range(COLB):
        cols = slice(cb * BLK, (cb + 1) * BLK)
        nv[:, cols] = 2.0 * returned(rec0, cb) + tv[:, cols]
    stored = pltpu.make_async_copy(nv, next_hbm, store_sem.at[0])
    stored.start()
    y_arrived(yw1, 1)
    for cb in range(COLB):
        cols = slice(cb * BLK, (cb + 1) * BLK)
        tv[:, cols] = 2.0 * (beta(yw1, cb) + dv[:, cols] * nv[:, cols]) - xv[:, cols]
    arrived_out(1)
    for cb in range(COLB):
        cols = slice(cb * BLK, (cb + 1) * BLK)
        ov[:, cols] = tv[:, cols] + 2.0 * returned(rec1, cb)
    last = pltpu.make_async_copy(ov, after_hbm, store_sem.at[1])
    last.start()

    for step in range(2):
        sent_in(step)
        pl.when(is_home)(lambda step=step: sent_out(step))
    y_sent(yw0, 0)
    y_sent(yw1, 1)
    stored.wait()
    last.wait()


def hand_over(next_in, after_in, next_out, after_out, held, sem):
    pairs = ((next_in, next_out), (after_in, after_out))
    taken = [pltpu.make_async_copy(c[0], held.at[k], sem.at[0, k]) for k, c in enumerate(pairs)]
    given = [pltpu.make_async_copy(held.at[k], c[1], sem.at[1, k]) for k, c in enumerate(pairs)]
    for c in taken:
        c.start()
    for k in range(2):
        taken[k].wait()
        given[k].start()
    for c in given:
        c.wait()


def on_device(prev, this, diag, ablk, acls, aoff, amask, bblk, bcls, boff, bmask):
    rows, columns = ROWS, COLB * BLK
    f32, bf16 = jnp.float32, jnp.bfloat16
    hbm = pl.BlockSpec(memory_space=pltpu.HBM)
    smem = pl.BlockSpec(memory_space=pltpu.SMEM)
    dma = pltpu.SemaphoreType.DMA
    next_vector, after_vector = pl.pallas_call(
        kernel,
        out_shape=[jax.ShapeDtypeStruct((rows, columns), f32)] * 2,
        in_specs=[hbm, hbm, hbm, hbm, smem, smem, smem, hbm, smem, smem, smem],
        out_specs=[hbm, hbm],
        scratch_shapes=[
            *[pltpu.VMEM((rows, columns), f32)] * 6,
            *[pltpu.VMEM((YWIN, TILES, TILE, BLK), bf16)] * 2,
            pltpu.VMEM((COLB, TILES, TILE, BLK), bf16),
            *[pltpu.VMEM((PIECES * TILES, TILE, BLK), bf16)] * 5,
            *[pltpu.VMEM((4, COLB, TILES, TILE, BLK), bf16)] * 2,
            pltpu.VMEM((WIN, 2, BLK, BLK), bf16),
            pltpu.VMEM((COLB, 2, BLK, BLK), bf16),
            pltpu.VMEM((WIN, BLK, 2 * BLK), bf16),
            pltpu.VMEM((COLB, BLK, 2 * BLK), bf16),
            dma((8,)),
            dma((2,)),
            *[dma((2, 4))] * 4,
            dma((2, 2, 4)),
            dma((4,)),
        ],
        compiler_params=pltpu.CompilerParams(
            collective_id=0, has_side_effects=True, vmem_limit_bytes=60 * 1024 * 1024
        ),
        name="chebyshev_steps",
    )(prev, this, diag, ablk, acls, aoff.T, amask.T, bblk, bcls, boff.T, bmask.T)
    return pl.pallas_call(
        hand_over,
        out_shape=[jax.ShapeDtypeStruct((rows, columns), f32)] * 2,
        in_specs=[hbm, hbm],
        out_specs=[hbm, hbm],
        scratch_shapes=[pltpu.VMEM((2, rows, columns), f32), dma((2, 2))],
        compiler_params=pltpu.CompilerParams(vmem_limit_bytes=60 * 1024 * 1024),
        name="hand_over",
    )(next_vector, after_vector)


def solution(mesh):
    own = P("aa", "ba")
    return jax.shard_map(
        on_device,
        mesh=mesh,
        in_specs=(own, own, own, *[P()] * 8),
        out_specs=(own, own),
        check_vma=False,
    )
```

```python
import jax
import jax.numpy as jnp
from jax import lax
from jax.experimental import pallas as pl
from jax.experimental.pallas import tpu as pltpu
from jax.sharding import PartitionSpec as P

BLK = 128
PLANES = 12
PLANE = 8
LINE = 8
ROWS = 48
COLB = 6
HOME = 2
ROWB = 3
WIN = 10
TILE = 16
TILES = 3
PARTS = ((0, 1), (1, 1), (2, 1))
PIECES = 27
YWIN = 24
NCLS = 8
MESH = pl.DeviceIdType.MESH


def remote(src, dst, send, recv, to):
    return pltpu.make_async_remote_copy(
        src_ref=src, dst_ref=dst, send_sem=send, recv_sem=recv, device_id=to, device_id_type=MESH
    )


def await_bytes(ref, sem):
    pltpu.make_async_copy(ref, ref, sem).wait()


def class_table(sizes):
    starts, lengths, first = [], [], jnp.int32(0)
    for c in range(NCLS):
        starts.append(first)
        lengths.append(sizes[c])
        first = first + sizes[c]
    return starts, lengths


def class_of(block, table):
    starts, lengths = table
    start, length = starts[0], lengths[0]
    for c in range(1, NCLS):
        later = block >= starts[c]
        start = jnp.where(later, starts[c], start)
        length = jnp.where(later, lengths[c], length)
    return start, length


def column_of(start, length, offset, halvings):
    for k in reversed(range(halvings)):
        step = length * (1 << k)
        offset = jnp.where(offset >= step, offset - step, offset)
    return start + offset


def kernel(
    prev_hbm, this_hbm, diag_hbm, ablk_hbm, acls, aoff, amask, bblk_hbm, bcls, boff, bmask,
    nv, ov,
    xv, pv, dv, tv, xb, yw1, pre, win0, wint, al0, al1, rec0, rec1, araw, braw, aw, bw,
    load_sem, in_send, in_recv, out_send, out_recv, y_sem, self_sem, *parts,
):
    yw0, tb = parts[: len(PARTS)], parts[len(PARTS) :]
    aa = lax.axis_index("aa")
    y = lax.axis_index("ba")
    z = lax.div(aa, PLANE)
    p = lax.rem(aa, PLANE)
    is_home = p >= HOME
    reaches = p < ROWB
    has_plane = {d: (z >= -d) if d < 0 else (z < PLANES - d) for d in (-2, -1, 1, 2)}
    has_line = {d: (y >= -d) if d < 0 else (y < LINE - d) for d in (-2, -1, 1, 2)}
    sends_far = jnp.logical_and(reaches, has_plane[-2])
    homes_far = jnp.logical_and(is_home, has_plane[2])

    def at(d, q):
        return {"aa": aa + (d * PLANE - p) + q, "ba": y}

    def along(d):
        return {"aa": aa, "ba": y + d}

    loads = [pltpu.make_async_copy(this_hbm, xv, load_sem.at[0])]
    loads[0].start()

    barrier = pltpu.get_barrier_semaphore()

    def greet(to):
        pl.semaphore_signal(barrier, inc=1, device_id=to, device_id_type=MESH)

    for d in (-2, -1, 1, 2):

        @pl.when(has_line[d])
        def _(d=d):
            greet(along(d))

    for d in (-1, 1):

        @pl.when(has_plane[d])
        def _(d=d):
            for q in range(PLANE):
                greet(at(d, q))

    for q in range(1, PLANE):
        greet(at(0, lax.rem(p + q, PLANE)))

    @pl.when(sends_far)
    def _():
        for cb in range(COLB):
            greet(at(-2, HOME + cb))

    @pl.when(homes_far)
    def _():
        for q in range(ROWB):
            greet(at(2, q))

    loads += [
        pltpu.make_async_copy(diag_hbm, dv, load_sem.at[1]),
        pltpu.make_async_copy(prev_hbm, pv, load_sem.at[2]),
        pltpu.make_async_copy(bblk_hbm.at[pl.ds(y * COLB, COLB)], braw, load_sem.at[3]),
    ]
    for k, (d, count) in enumerate(((-1, ROWB), (0, ROWB), (1, ROWB), (2, 1))):
        held = lax.rem(z + d + PLANES, PLANES)
        loads.append(
            pltpu.make_async_copy(
                ablk_hbm.at[pl.ds(held * ROWB, count)],
                araw.at[pl.ds(ROWB * k, count)],
                load_sem.at[4 + k],
            )
        )
    for c in loads[1:]:
        c.start()

    loads[0].wait()
    for cb in range(COLB):
        own = xv[:, cb * BLK : (cb + 1) * BLK].astype(jnp.bfloat16).reshape(TILES, TILE, BLK)
        xb[cb] = own
        for k, (tile, tiles) in enumerate(PARTS):
            yw0[k][9 + cb] = own[tile : tile + tiles]

    greetings = PLANE - 1 + jnp.where(sends_far, COLB, 0) + jnp.where(homes_far, ROWB, 0)
    for d in (-2, -1, 1, 2):
        greetings = greetings + jnp.where(has_line[d], 1, 0)
    for d in (-1, 1):
        greetings = greetings + jnp.where(has_plane[d], PLANE, 0)
    pl.semaphore_wait(barrier, greetings)

    def y_copy(w, at_sem, k):
        src, n, dst, d = ((9, 6, 3, 1), (9, 6, 15, -1), (12, 3, 0, 2), (9, 3, 21, -2))[k]
        return d, remote(
            w.at[pl.ds(src, n)], w.at[pl.ds(dst, n)],
            y_sem.at[at_sem, 0, k], y_sem.at[at_sem, 1, k], along(d),
        )

    def y_start(w, at_sem):
        for k in range(4):
            d, copy = y_copy(w, at_sem, k)
            pl.when(has_line[d])(copy.start)

    def y_sent(w, at_sem):
        for k in range(4):
            d, copy = y_copy(w, at_sem, k)
            pl.when(has_line[d])(copy.wait_send)

    def y_arrived(w, at_sem):
        for k in range(4):
            d, copy = y_copy(w, at_sem, k)
            pl.when(has_line[-d])(copy.wait_recv)

    def piece(k):
        return pl.ds(TILES * k, TILES)

    def send_in(src, w, step, cb, tile, tiles):
        to = HOME + cb

        def place(k):
            return w.at[pl.ds(TILES * k + tile, tiles)]

        @pl.when(sends_far)
        def _():
            remote(
                src, place(3 * PLANE + p),
                in_send.at[step, 3], in_recv.at[step, 3], at(-2, to),
            ).start()

        for k, d, base in ((2, -1, 2 * PLANE), (0, 1, 0)):

            @pl.when(has_plane[d])
            def _(k=k, d=d, base=base):
                remote(
                    src, place(base + p),
                    in_send.at[step, k], in_recv.at[step, k], at(d, to),
                ).start()

        @pl.when(p != to)
        def _():
            remote(
                src, place(PLANE + p), in_send.at[step, 1], in_recv.at[step, 1], at(0, to)
            ).start()

        @pl.when(p == to)
        def _():
            pltpu.make_async_copy(src, place(PLANE + p), self_sem.at[step]).start()

    def await_pieces(count, sem):
        await_bytes(win0.at[pl.ds(0, count * TILES)], sem)

    def sent_in(step):
        pl.when(sends_far)(lambda: await_pieces(COLB, in_send.at[step, 3]))
        pl.when(has_plane[-1])(lambda: await_pieces(COLB, in_send.at[step, 2]))
        pl.when(has_plane[1])(lambda: await_pieces(COLB, in_send.at[step, 0]))
        pl.when(is_home)(lambda: await_pieces(COLB - 1, in_send.at[step, 1]))
        pl.when(jnp.logical_not(is_home))(lambda: await_pieces(COLB, in_send.at[step, 1]))

    def arrived_in(step):
        await_pieces(1, self_sem.at[step])
        await_pieces(PLANE - 1, in_recv.at[step, 1])
        pl.when(has_plane[-1])(lambda: await_pieces(PLANE, in_recv.at[step, 0]))
        pl.when(has_plane[1])(lambda: await_pieces(PLANE, in_recv.at[step, 2]))
        pl.when(has_plane[2])(lambda: await_pieces(ROWB, in_recv.at[step, 3]))

    def send_out(src, rec, step, d, base, slot, count):
        @pl.when(has_plane[d])
        def _():
            for q in range(count):
                remote(
                    src.at[piece(base + q)], rec.at[slot, p - HOME],
                    out_send.at[step, slot], out_recv.at[step, slot], at(d, q),
                ).start()

    def send_own(src, rec, step):
        for k in range(1, PLANE):
            q = lax.rem(p + k, PLANE)
            remote(
                src.at[piece(PLANE + q)], rec.at[1, p - HOME],
                out_send.at[step, 1], out_recv.at[step, 1], at(0, q),
            ).start()
        pltpu.make_async_copy(
            src.at[piece(PLANE + p)], rec.at[1, p - HOME], self_sem.at[2 + step]
        ).start()

    def sent_out(step):
        await_pieces(PLANE - 1, out_send.at[step, 1])
        pl.when(has_plane[2])(lambda: await_pieces(ROWB, out_send.at[step, 3]))
        pl.when(has_plane[1])(lambda: await_pieces(PLANE, out_send.at[step, 0]))
        pl.when(has_plane[-1])(lambda: await_pieces(PLANE, out_send.at[step, 2]))

    def arrived_out(step):
        pl.when(sends_far)(lambda: await_pieces(COLB, out_recv.at[step, 3]))
        pl.when(has_plane[-1])(lambda: await_pieces(COLB, out_recv.at[step, 0]))
        pl.when(has_plane[1])(lambda: await_pieces(COLB, out_recv.at[step, 2]))
        pl.when(jnp.logical_not(is_home))(lambda: await_pieces(COLB, out_recv.at[step, 1]))

        @pl.when(is_home)
        def _():
            await_pieces(COLB - 1, out_recv.at[step, 1])
            await_pieces(1, self_sem.at[2 + step])

    for k in range(len(PARTS)):
        y_start(yw0[k], k)
    for cb in range(COLB):
        send_in(xb.at[cb], win0, 0, cb, 0, TILES)

    a_table = class_table(acls)
    b_table = class_table(bcls)
    a_at = []
    for j in range(WIN):
        block = lax.rem(z * ROWB - ROWB + j + PLANES * ROWB, PLANES * ROWB)
        start, length = class_of(block, a_table)
        a_at.append(
            [
                jnp.clip(
                    column_of(start, length, aoff[k, block], 3) - (z - 1) * ROWB, 0, WIN - 1
                )
                for k in range(2)
            ]
        )
    b_at = []
    for r in range(COLB):
        block = y * COLB + r
        start, length = class_of(block, b_table)
        b_at.append(
            [
                jnp.clip(
                    column_of(start, length, boff[k, block], 4) - y * COLB + 9, 0, YWIN - 1
                )
                for k in range(2)
            ]
        )
    slot_at = []
    for q in range(3):
        start, length = class_of(z * ROWB + lax.div(3 * p + q, PLANE), a_table)
        middle = start + lax.div(length - 1, 2)
        away = lax.div(middle, ROWB) - z
        slot_at.append(jnp.clip(jnp.where(away == -2, 3, away + 1), 0, 3))

    for c in loads[1:]:
        c.wait()
    for r in range(COLB):
        for k in range(2):
            live = bmask[k, y * COLB + r].astype(jnp.float32)
            bw[r, :, k * BLK : (k + 1) * BLK] = (braw[r, k].astype(jnp.float32) * live).astype(
                jnp.bfloat16
            )

    @pl.when(is_home)
    def _():
        for j in range(WIN):
            block = lax.rem(z * ROWB - ROWB + j + PLANES * ROWB, PLANES * ROWB)
            for k in range(2):
                live = amask[k, block].astype(jnp.float32)
                aw[j, :, k * BLK : (k + 1) * BLK] = (
                    araw[j, k].astype(jnp.float32) * live
                ).astype(jnp.bfloat16)
        al0[8 * WIN] = jnp.zeros((TILE, BLK), jnp.bfloat16)
        al1[8 * WIN] = jnp.zeros((TILE, BLK), jnp.bfloat16)

    def beta(w, r, rows):
        both = jnp.concatenate([w[b_at[r][k]].reshape(rows, BLK) for k in range(2)], axis=1)
        return lax.dot_general(
            both, bw[r], (((1,), (1,)), ((), ())), preferred_element_type=jnp.float32
        )

    def couple(w, j):
        both = jnp.concatenate(
            [w[pl.ds(a_at[j][k] * 8, 8)].reshape(BLK, BLK) for k in range(2)], axis=0
        )
        return jnp.dot(aw[j], both, preferred_element_type=jnp.float32)

    def alpha(w, out, rows, more):
        for j in rows:
            product = couple(w, j)
            if more:
                product = product + pre[j]
            out[8 * j : 8 * (j + 1)] = product.astype(jnp.bfloat16).reshape(8, TILE, BLK)

    def alpha_and_send(w, out, rec, step, more):
        alpha(w, out, range(9, 10), more)
        send_out(out, rec, step, 2, 3 * PLANE, 3, ROWB)
        alpha(w, out, range(6, 9), more)
        send_out(out, rec, step, 1, 2 * PLANE, 0, PLANE)
        alpha(w, out, range(0, 3), more)
        send_out(out, rec, step, -1, 0, 2, PLANE)
        alpha(w, out, range(3, 6), more)
        send_own(out, rec, step)

    def returned(rec, cb):
        return jnp.concatenate(
            [rec[slot_at[q], cb, q] for q in range(TILES)], axis=0
        ).astype(jnp.float32)

    for k, (tile, tiles) in enumerate(PARTS):
        rows = slice(TILE * tile, TILE * (tile + tiles))
        y_arrived(yw0[k], k)
        for cb in range(COLB):
            cols = slice(cb * BLK, (cb + 1) * BLK)
            b1 = beta(yw0[k], cb, TILE * tiles).astype(jnp.bfloat16).astype(jnp.float32)
            t = 2.0 * (b1 + dv[rows, cols] * xv[rows, cols]) - pv[rows, cols]
            tv[rows, cols] = t
            yw1[9 + cb, tile : tile + tiles] = t.astype(jnp.bfloat16).reshape(tiles, TILE, BLK)
            tb[k][cb] = (t + 2.0 * b1).astype(jnp.bfloat16).reshape(tiles, TILE, BLK)
            send_in(tb[k].at[cb], wint, 1, cb, tile, tiles)
    y_start(yw1, len(PARTS))

    @pl.when(is_home)
    def _():
        arrived_in(0)
        alpha_and_send(win0, al0, rec0, 0, False)
        for j in range(WIN):
            pre[j] = 2.0 * couple(al0, j)
        arrived_in(1)
        alpha_and_send(wint, al1, rec1, 1, True)

    arrived_out(0)
    for cb in range(COLB):
        cols = slice(cb * BLK, (cb + 1) * BLK)
        nv[:, cols] = 2.0 * returned(rec0, cb) + tv[:, cols]
    y_arrived(yw1, len(PARTS))
    for cb in range(COLB):
        cols = slice(cb * BLK, (cb + 1) * BLK)
        tv[:, cols] = 2.0 * (beta(yw1, cb, ROWS) + dv[:, cols] * nv[:, cols]) - xv[:, cols]
    arrived_out(1)
    for cb in range(COLB):
        cols = slice(cb * BLK, (cb + 1) * BLK)
        ov[:, cols] = tv[:, cols] + 2.0 * returned(rec1, cb)

    for step in range(2):
        sent_in(step)
        pl.when(is_home)(lambda step=step: sent_out(step))
    for k in range(len(PARTS)):
        y_sent(yw0[k], k)
    y_sent(yw1, len(PARTS))


def hand_over(next_in, after_in, next_out, after_out, sem):
    copies = [
        pltpu.make_async_copy(next_in, next_out, sem.at[0]),
        pltpu.make_async_copy(after_in, after_out, sem.at[1]),
    ]
    for c in copies:
        c.start()
    for c in copies:
        c.wait()


def on_device(prev, this, diag, ablk, acls, aoff, amask, bblk, bcls, boff, bmask):
    rows, columns = ROWS, COLB * BLK
    f32, bf16 = jnp.float32, jnp.bfloat16
    hbm = pl.BlockSpec(memory_space=pltpu.HBM)
    vmem = pl.BlockSpec(memory_space=pltpu.VMEM)
    smem = pl.BlockSpec(memory_space=pltpu.SMEM)
    dma = pltpu.SemaphoreType.DMA
    next_vector, after_vector = pl.pallas_call(
        kernel,
        out_shape=[pltpu.VMEM((rows, columns), f32)] * 2,
        in_specs=[hbm, hbm, hbm, hbm, smem, smem, smem, hbm, smem, smem, smem],
        out_specs=[vmem, vmem],
        scratch_shapes=[
            *[pltpu.VMEM((rows, columns), f32)] * 4,
            pltpu.VMEM((COLB, TILES, TILE, BLK), bf16),
            pltpu.VMEM((YWIN, TILES, TILE, BLK), bf16),
            pltpu.VMEM((WIN, BLK, BLK), f32),
            *[pltpu.VMEM((PIECES * TILES, TILE, BLK), bf16)] * 4,
            *[pltpu.VMEM((4, COLB, TILES, TILE, BLK), bf16)] * 2,
            pltpu.VMEM((WIN, 2, BLK, BLK), bf16),
            pltpu.VMEM((COLB, 2, BLK, BLK), bf16),
            pltpu.VMEM((WIN, BLK, 2 * BLK), bf16),
            pltpu.VMEM((COLB, BLK, 2 * BLK), bf16),
            dma((8,)),
            *[dma((2, 4))] * 4,
            dma((1 + len(PARTS), 2, 4)),
            dma((4,)),
            *[pltpu.VMEM((YWIN, tiles, TILE, BLK), bf16) for _, tiles in PARTS],
            *[pltpu.VMEM((COLB, tiles, TILE, BLK), bf16) for _, tiles in PARTS],
        ],
        compiler_params=pltpu.CompilerParams(
            collective_id=0, has_side_effects=True, vmem_limit_bytes=60 * 1024 * 1024
        ),
        name="chebyshev_steps",
    )(prev, this, diag, ablk, acls, aoff.T, amask.T, bblk, bcls, boff.T, bmask.T)
    return pl.pallas_call(
        hand_over,
        out_shape=[jax.ShapeDtypeStruct((rows, columns), f32)] * 2,
        in_specs=[pl.BlockSpec(memory_space=pl.ANY)] * 2,
        out_specs=[hbm, hbm],
        scratch_shapes=[dma((2,))],
        compiler_params=pltpu.CompilerParams(vmem_limit_bytes=1024 * 1024),
        name="hand_over",
    )(next_vector, after_vector)


def solution(mesh):
    own = P("aa", "ba")
    return jax.shard_map(
        on_device,
        mesh=mesh,
        in_specs=(own, own, own, *[P()] * 8),
        out_specs=(own, own),
        check_vma=False,
    )
```

```python
import jax
import jax.numpy as jnp
from jax import lax
from jax.experimental import pallas as pl
from jax.experimental.pallas import tpu as pltpu
from jax.sharding import PartitionSpec as P

BLK = 128
PLANES = 12
PLANE = 8
LINE = 8
ROWS = 48
COLB = 6
HOME = 2
ROWB = 3
WIN = 10
TILE = 16
TILES = 3
PARTS = ((0, 1), (1, 1), (2, 1))
BTILES = 8
FAR = 72
YWIN = 24
NCLS = 8
MESH = pl.DeviceIdType.MESH


def remote(src, dst, send, recv, to):
    return pltpu.make_async_remote_copy(
        src_ref=src, dst_ref=dst, send_sem=send, recv_sem=recv, device_id=to, device_id_type=MESH
    )


def await_bytes(ref, sem):
    pltpu.make_async_copy(ref, ref, sem).wait()


def class_table(sizes):
    starts, lengths, first = [], [], jnp.int32(0)
    for c in range(NCLS):
        starts.append(first)
        lengths.append(sizes[c])
        first = first + sizes[c]
    return starts, lengths


def class_of(block, table):
    starts, lengths = table
    start, length = starts[0], lengths[0]
    for c in range(1, NCLS):
        later = block >= starts[c]
        start = jnp.where(later, starts[c], start)
        length = jnp.where(later, lengths[c], length)
    return start, length


def column_of(start, length, offset, halvings):
    for k in reversed(range(halvings)):
        step = length * (1 << k)
        offset = jnp.where(offset >= step, offset - step, offset)
    return start + offset


def kernel(
    prev_hbm, this_hbm, diag_hbm, ablk_hbm, acls, aoff, amask, bblk_hbm, bcls, boff, bmask,
    nv, ov,
    xv, pv, dv, tv, xb, yw1, pre, win0, wint, al0, al1, rec0, rec1, araw, braw, aw, bw,
    load_sem, in_send, in_recv, out_send, out_recv, y_sem, self_sem, *parts,
):
    yw0, tb = parts[: len(PARTS)], parts[len(PARTS) :]
    aa = lax.axis_index("aa")
    y = lax.axis_index("ba")
    z = lax.div(aa, PLANE)
    p = lax.rem(aa, PLANE)
    is_home = p >= HOME
    odd = lax.rem(p, 2) == 1
    has_plane = {d: (z >= -d) if d < 0 else (z < PLANES - d) for d in (-2, -1, 1, 2)}
    has_line = {d: (y >= -d) if d < 0 else (y < LINE - d) for d in (-2, -1, 1, 2)}
    sides = ((-2, 0, 0, 0), (2, 1, PLANE - ROWB, 1))
    in_far = {
        d: jnp.logical_and(p < ROWB if parity == 0 else p >= PLANE - ROWB, has_plane[d])
        for d, parity, _, _ in sides
    }
    home_far = {
        d: jnp.logical_and(jnp.logical_and(is_home, odd if parity else jnp.logical_not(odd)), has_plane[-d])
        for d, parity, _, _ in sides
    }

    def far_tiles(q, skip):
        return [(k, TILES * q + k - skip) for k in range(TILES) if 0 <= TILES * q + k - skip < BTILES]

    def at(d, q):
        return {"aa": aa + (d * PLANE - p) + q, "ba": y}

    def along(d):
        return {"aa": aa, "ba": y + d}

    loads = [pltpu.make_async_copy(this_hbm, xv, load_sem.at[0])]
    loads[0].start()

    barrier = pltpu.get_barrier_semaphore()

    def greet(to):
        pl.semaphore_signal(barrier, inc=1, device_id=to, device_id_type=MESH)

    for d in (-2, -1, 1, 2):

        @pl.when(has_line[d])
        def _(d=d):
            greet(along(d))

    for d in (-1, 1):

        @pl.when(has_plane[d])
        def _(d=d):
            for q in range(PLANE):
                greet(at(d, q))

    for q in range(1, PLANE):
        greet(at(0, lax.rem(p + q, PLANE)))

    for d, parity, low, _ in sides:

        @pl.when(in_far[d])
        def _(d=d, parity=parity):
            for cb in range(parity, COLB, 2):
                greet(at(d, HOME + cb))

        @pl.when(home_far[d])
        def _(d=d, low=low):
            for q in range(ROWB):
                greet(at(-d, low + q))

    loads += [
        pltpu.make_async_copy(diag_hbm, dv, load_sem.at[1]),
        pltpu.make_async_copy(prev_hbm, pv, load_sem.at[2]),
        pltpu.make_async_copy(bblk_hbm.at[pl.ds(y * COLB, COLB)], braw, load_sem.at[3]),
    ]
    blocks = PLANES * ROWB
    a_block = [lax.rem(z * ROWB - ROWB + j + blocks, blocks) for j in range(WIN - 1)]
    a_block.append(lax.rem(z * ROWB + jnp.where(odd, blocks - 4, 2 * ROWB), blocks))
    for k, (j, count) in enumerate(((0, ROWB), (ROWB, ROWB), (2 * ROWB, ROWB), (3 * ROWB, 1))):
        loads.append(
            pltpu.make_async_copy(
                ablk_hbm.at[pl.ds(a_block[j], count)], araw.at[pl.ds(j, count)], load_sem.at[4 + k]
            )
        )

    loads[0].wait()
    for cb in range(COLB):
        own = xv[:, cb * BLK : (cb + 1) * BLK].astype(jnp.bfloat16).reshape(TILES, TILE, BLK)
        xb[cb] = own
        for k, (tile, tiles) in enumerate(PARTS):
            yw0[k][9 + cb] = own[tile : tile + tiles]

    greetings = PLANE - 1
    for d, _, _, _ in sides:
        greetings = greetings + jnp.where(in_far[d], COLB // 2, 0) + jnp.where(home_far[d], ROWB, 0)
    for d in (-2, -1, 1, 2):
        greetings = greetings + jnp.where(has_line[d], 1, 0)
    for d in (-1, 1):
        greetings = greetings + jnp.where(has_plane[d], PLANE, 0)
    pl.semaphore_wait(barrier, greetings)

    def y_copy(w, at_sem, k):
        src, n, dst, d = ((9, 6, 3, 1), (9, 6, 15, -1), (12, 3, 0, 2), (9, 3, 21, -2))[k]
        return d, remote(
            w.at[pl.ds(src, n)], w.at[pl.ds(dst, n)],
            y_sem.at[at_sem, 0, k], y_sem.at[at_sem, 1, k], along(d),
        )

    def y_start(w, at_sem):
        for k in range(4):
            d, copy = y_copy(w, at_sem, k)
            pl.when(has_line[d])(copy.start)

    def y_sent(w, at_sem):
        for k in range(4):
            d, copy = y_copy(w, at_sem, k)
            pl.when(has_line[d])(copy.wait_send)

    def y_arrived(w, at_sem):
        for k in range(4):
            d, copy = y_copy(w, at_sem, k)
            pl.when(has_line[-d])(copy.wait_recv)

    def piece(k):
        return pl.ds(TILES * k, TILES)

    def send_in(src, w, step, cb, tile, tiles):
        to = HOME + cb

        def place(k):
            return w.at[pl.ds(TILES * k + tile, tiles)]

        d, _, low, skip = sides[cb % 2]

        for q in range(ROWB):
            spots = [(k, spot) for k, spot in far_tiles(q, skip) if tile <= k < tile + tiles]
            if spots:

                @pl.when(jnp.logical_and(p == low + q, has_plane[d]))
                def _(spots=spots):
                    remote(
                        src.at[pl.ds(spots[0][0] - tile, len(spots))],
                        w.at[pl.ds(FAR + spots[0][1], len(spots))],
                        in_send.at[step, 3], in_recv.at[step, 3], at(d, to),
                    ).start()

        for k, d, base in ((2, -1, 2 * PLANE), (0, 1, 0)):

            @pl.when(has_plane[d])
            def _(k=k, d=d, base=base):
                remote(
                    src, place(base + p),
                    in_send.at[step, k], in_recv.at[step, k], at(d, to),
                ).start()

        @pl.when(p != to)
        def _():
            remote(
                src, place(PLANE + p), in_send.at[step, 1], in_recv.at[step, 1], at(0, to)
            ).start()

        @pl.when(p == to)
        def _():
            pltpu.make_async_copy(src, place(PLANE + p), self_sem.at[step]).start()

    def await_pieces(count, sem):
        await_bytes(win0.at[pl.ds(0, count * TILES)], sem)

    def await_far_rows(sem):
        for d, _, low, skip in sides:
            for q in range(ROWB):
                count = COLB // 2 * len(far_tiles(q, skip))

                @pl.when(jnp.logical_and(p == low + q, has_plane[d]))
                def _(count=count):
                    await_bytes(win0.at[pl.ds(0, count)], sem)

    def await_far_block(sem):
        for d, _, _, _ in sides:
            pl.when(home_far[d])(lambda: await_bytes(win0.at[pl.ds(0, BTILES)], sem))

    def sent_in(step):
        await_far_rows(in_send.at[step, 3])
        pl.when(has_plane[-1])(lambda: await_pieces(COLB, in_send.at[step, 2]))
        pl.when(has_plane[1])(lambda: await_pieces(COLB, in_send.at[step, 0]))
        pl.when(is_home)(lambda: await_pieces(COLB - 1, in_send.at[step, 1]))
        pl.when(jnp.logical_not(is_home))(lambda: await_pieces(COLB, in_send.at[step, 1]))

    def arrived_in(step):
        await_pieces(1, self_sem.at[step])
        await_pieces(PLANE - 1, in_recv.at[step, 1])
        pl.when(has_plane[-1])(lambda: await_pieces(PLANE, in_recv.at[step, 0]))
        pl.when(has_plane[1])(lambda: await_pieces(PLANE, in_recv.at[step, 2]))
        await_far_block(in_recv.at[step, 3])

    def send_far(src, rec, step):
        for d, _, low, skip in sides:

            @pl.when(home_far[d])
            def _(d=d, low=low, skip=skip):
                for q in range(ROWB):
                    spots = far_tiles(q, skip)
                    remote(
                        src.at[pl.ds(FAR + spots[0][1], len(spots))],
                        rec.at[3, p - HOME, pl.ds(spots[0][0], len(spots))],
                        out_send.at[step, 3], out_recv.at[step, 3], at(-d, low + q),
                    ).start()

    def send_out(src, rec, step, d, base, slot):
        @pl.when(has_plane[d])
        def _():
            for q in range(PLANE):
                remote(
                    src.at[piece(base + q)], rec.at[slot, p - HOME],
                    out_send.at[step, slot], out_recv.at[step, slot], at(d, q),
                ).start()

    def send_own(src, rec, step):
        for k in range(1, PLANE):
            q = lax.rem(p + k, PLANE)
            remote(
                src.at[piece(PLANE + q)], rec.at[1, p - HOME],
                out_send.at[step, 1], out_recv.at[step, 1], at(0, q),
            ).start()
        pltpu.make_async_copy(
            src.at[piece(PLANE + p)], rec.at[1, p - HOME], self_sem.at[2 + step]
        ).start()

    def sent_out(step):
        await_pieces(PLANE - 1, out_send.at[step, 1])
        await_far_block(out_send.at[step, 3])
        pl.when(has_plane[1])(lambda: await_pieces(PLANE, out_send.at[step, 0]))
        pl.when(has_plane[-1])(lambda: await_pieces(PLANE, out_send.at[step, 2]))

    def arrived_out(step):
        await_far_rows(out_recv.at[step, 3])
        pl.when(has_plane[-1])(lambda: await_pieces(COLB, out_recv.at[step, 0]))
        pl.when(has_plane[1])(lambda: await_pieces(COLB, out_recv.at[step, 2]))
        pl.when(jnp.logical_not(is_home))(lambda: await_pieces(COLB, out_recv.at[step, 1]))

        @pl.when(is_home)
        def _():
            await_pieces(COLB - 1, out_recv.at[step, 1])
            await_pieces(1, self_sem.at[2 + step])

    for k in range(len(PARTS)):
        y_start(yw0[k], k)
    for cb in range(COLB):
        send_in(xb.at[cb], win0, 0, cb, 0, TILES)
    for c in loads[1:]:
        c.start()

    a_table = class_table(acls)
    b_table = class_table(bcls)
    a_at = []
    for j in range(WIN):
        start, length = class_of(a_block[j], a_table)
        spots = []
        for k in range(2):
            spot = column_of(start, length, aoff[k, a_block[j]], 3) - (z - 1) * ROWB
            spots.append(jnp.where(spot < 0, WIN - 1, jnp.minimum(spot, WIN - 1)))
        a_at.append(spots)
    b_at = []
    for r in range(COLB):
        block = y * COLB + r
        start, length = class_of(block, b_table)
        b_at.append(
            [
                jnp.clip(
                    column_of(start, length, boff[k, block], 4) - y * COLB + 9, 0, YWIN - 1
                )
                for k in range(2)
            ]
        )
    slot_at = []
    for parity in range(2):
        slots = []
        for q in range(TILES):
            start, length = class_of(z * ROWB + lax.div(TILES * p + q, PLANE), a_table)
            away = lax.div(start + lax.div(length - 1 + parity, 2), ROWB) - z
            slot = jnp.where(jnp.logical_or(away < -1, away > 1), 3, away + 1)
            slots.append(jnp.clip(slot, 0, 3))
        slot_at.append(slots)

    for c in loads[1:]:
        c.wait()
    for r in range(COLB):
        for k in range(2):
            live = bmask[k, y * COLB + r].astype(jnp.float32)
            bw[r, :, k * BLK : (k + 1) * BLK] = (braw[r, k].astype(jnp.float32) * live).astype(
                jnp.bfloat16
            )

    @pl.when(is_home)
    def _():
        for j in range(WIN):
            for k in range(2):
                live = amask[k, a_block[j]].astype(jnp.float32)
                aw[j, :, k * BLK : (k + 1) * BLK] = (
                    araw[j, k].astype(jnp.float32) * live
                ).astype(jnp.bfloat16)

    def beta(w, r, rows):
        both = jnp.concatenate([w[b_at[r][k]].reshape(rows, BLK) for k in range(2)], axis=1)
        return lax.dot_general(
            both, bw[r], (((1,), (1,)), ((), ())), preferred_element_type=jnp.float32
        )

    def couple(w, j):
        both = jnp.concatenate(
            [w[pl.ds(a_at[j][k] * 8, 8)].reshape(BLK, BLK) for k in range(2)], axis=0
        )
        return jnp.dot(aw[j], both, preferred_element_type=jnp.float32)

    def alpha(w, out, rows, more):
        for j in rows:
            product = couple(w, j)
            if more:
                product = product + pre[j]
            out[8 * j : 8 * (j + 1)] = product.astype(jnp.bfloat16).reshape(8, TILE, BLK)

    def alpha_and_send(w, out, rec, step, more):
        alpha(w, out, range(9, 10), more)
        send_far(out, rec, step)
        alpha(w, out, range(6, 9), more)
        send_out(out, rec, step, 1, 2 * PLANE, 0)
        alpha(w, out, range(0, 3), more)
        send_out(out, rec, step, -1, 0, 2)
        alpha(w, out, range(3, 6), more)
        send_own(out, rec, step)

    def returned(rec, cb):
        return jnp.concatenate(
            [rec[slot_at[cb % 2][q], cb, q] for q in range(TILES)], axis=0
        ).astype(jnp.float32)

    for k, (tile, tiles) in enumerate(PARTS):
        rows = slice(TILE * tile, TILE * (tile + tiles))
        y_arrived(yw0[k], k)
        for cb in range(COLB):
            cols = slice(cb * BLK, (cb + 1) * BLK)
            b1 = beta(yw0[k], cb, TILE * tiles).astype(jnp.bfloat16).astype(jnp.float32)
            t = 2.0 * (b1 + dv[rows, cols] * xv[rows, cols]) - pv[rows, cols]
            tv[rows, cols] = t
            yw1[9 + cb, tile : tile + tiles] = t.astype(jnp.bfloat16).reshape(tiles, TILE, BLK)
            tb[k][cb] = (t + 2.0 * b1).astype(jnp.bfloat16).reshape(tiles, TILE, BLK)
            send_in(tb[k].at[cb], wint, 1, cb, tile, tiles)
    y_start(yw1, len(PARTS))

    @pl.when(is_home)
    def _():
        arrived_in(0)
        alpha_and_send(win0, al0, rec0, 0, False)
        for j in range(WIN):
            pre[j] = 2.0 * couple(al0, j)
        arrived_in(1)
        alpha_and_send(wint, al1, rec1, 1, True)

    arrived_out(0)
    for cb in range(COLB):
        cols = slice(cb * BLK, (cb + 1) * BLK)
        nv[:, cols] = 2.0 * returned(rec0, cb) + tv[:, cols]
    y_arrived(yw1, len(PARTS))
    for cb in range(COLB):
        cols = slice(cb * BLK, (cb + 1) * BLK)
        tv[:, cols] = 2.0 * (beta(yw1, cb, ROWS) + dv[:, cols] * nv[:, cols]) - xv[:, cols]
    arrived_out(1)
    for cb in range(COLB):
        cols = slice(cb * BLK, (cb + 1) * BLK)
        ov[:, cols] = tv[:, cols] + 2.0 * returned(rec1, cb)

    for step in range(2):
        sent_in(step)
        pl.when(is_home)(lambda step=step: sent_out(step))
    for k in range(len(PARTS)):
        y_sent(yw0[k], k)
    y_sent(yw1, len(PARTS))


def hand_over(next_in, after_in, next_out, after_out, sem):
    copies = [
        pltpu.make_async_copy(next_in, next_out, sem.at[0]),
        pltpu.make_async_copy(after_in, after_out, sem.at[1]),
    ]
    for c in copies:
        c.start()
    for c in copies:
        c.wait()


def on_device(prev, this, diag, ablk, acls, aoff, amask, bblk, bcls, boff, bmask):
    rows, columns = ROWS, COLB * BLK
    f32, bf16 = jnp.float32, jnp.bfloat16
    hbm = pl.BlockSpec(memory_space=pltpu.HBM)
    vmem = pl.BlockSpec(memory_space=pltpu.VMEM)
    smem = pl.BlockSpec(memory_space=pltpu.SMEM)
    dma = pltpu.SemaphoreType.DMA
    next_vector, after_vector = pl.pallas_call(
        kernel,
        out_shape=[pltpu.VMEM((rows, columns), f32)] * 2,
        in_specs=[hbm, hbm, hbm, hbm, smem, smem, smem, hbm, smem, smem, smem],
        out_specs=[vmem, vmem],
        scratch_shapes=[
            *[pltpu.VMEM((rows, columns), f32)] * 4,
            pltpu.VMEM((COLB, TILES, TILE, BLK), bf16),
            pltpu.VMEM((YWIN, TILES, TILE, BLK), bf16),
            pltpu.VMEM((WIN, BLK, BLK), f32),
            *[pltpu.VMEM((WIN * BTILES, TILE, BLK), bf16)] * 4,
            *[pltpu.VMEM((4, COLB, TILES, TILE, BLK), bf16)] * 2,
            pltpu.VMEM((WIN, 2, BLK, BLK), bf16),
            pltpu.VMEM((COLB, 2, BLK, BLK), bf16),
            pltpu.VMEM((WIN, BLK, 2 * BLK), bf16),
            pltpu.VMEM((COLB, BLK, 2 * BLK), bf16),
            dma((8,)),
            *[dma((2, 4))] * 4,
            dma((1 + len(PARTS), 2, 4)),
            dma((4,)),
            *[pltpu.VMEM((YWIN, tiles, TILE, BLK), bf16) for _, tiles in PARTS],
            *[pltpu.VMEM((COLB, tiles, TILE, BLK), bf16) for _, tiles in PARTS],
        ],
        compiler_params=pltpu.CompilerParams(
            collective_id=0, has_side_effects=True, vmem_limit_bytes=60 * 1024 * 1024
        ),
        name="chebyshev_steps",
    )(prev, this, diag, ablk, acls, aoff.T, amask.T, bblk, bcls, boff.T, bmask.T)
    return pl.pallas_call(
        hand_over,
        out_shape=[jax.ShapeDtypeStruct((rows, columns), f32)] * 2,
        in_specs=[pl.BlockSpec(memory_space=pl.ANY)] * 2,
        out_specs=[hbm, hbm],
        scratch_shapes=[dma((2,))],
        compiler_params=pltpu.CompilerParams(vmem_limit_bytes=1024 * 1024),
        name="hand_over",
    )(next_vector, after_vector)


def solution(mesh):
    own = P("aa", "ba")
    return jax.shard_map(
        on_device,
        mesh=mesh,
        in_specs=(own, own, own, *[P()] * 8),
        out_specs=(own, own),
        check_vma=False,
    )
```

```python
import jax
import jax.numpy as jnp
from jax import lax
from jax.experimental import pallas as pl
from jax.experimental.pallas import tpu as pltpu
from jax.sharding import PartitionSpec as P

BLK = 128
PLANES = 12
PLANE = 8
LINE = 8
ROWS = 48
COLB = 6
HOME = 2
ROWB = 3
WIN = 10
TILE = 16
TILES = 3
PARTS = ((0, 1), (1, 1), (2, 1))
BTILES = 8
FAR = 72
YWIN = 24
NCLS = 8
MESH = pl.DeviceIdType.MESH


def remote(src, dst, send, recv, to):
    return pltpu.make_async_remote_copy(
        src_ref=src, dst_ref=dst, send_sem=send, recv_sem=recv, device_id=to, device_id_type=MESH
    )


def await_bytes(ref, sem):
    pltpu.make_async_copy(ref, ref, sem).wait()


def class_table(sizes):
    starts, lengths, first = [], [], jnp.int32(0)
    for c in range(NCLS):
        starts.append(first)
        lengths.append(sizes[c])
        first = first + sizes[c]
    return starts, lengths


def class_of(block, table):
    starts, lengths = table
    start, length = starts[0], lengths[0]
    for c in range(1, NCLS):
        later = block >= starts[c]
        start = jnp.where(later, starts[c], start)
        length = jnp.where(later, lengths[c], length)
    return start, length


def column_of(start, length, offset, halvings):
    for k in reversed(range(halvings)):
        step = length * (1 << k)
        offset = jnp.where(offset >= step, offset - step, offset)
    return start + offset


def kernel(
    prev_hbm, this_hbm, diag_hbm, ablk_hbm, acls, aoff, amask, bblk_hbm, bcls, boff, bmask,
    nv, ov,
    xv, pv, dv, tv, xb, yw1, pre, win0, wint, al0, al1, rec0, rec1, araw, braw, aw, bw,
    load_sem, in_send, in_recv, out_send, out_recv, y_sem, self_sem, *parts,
):
    yw0, tb = parts[: len(PARTS)], parts[len(PARTS) :]
    aa = lax.axis_index("aa")
    y = lax.axis_index("ba")
    z = lax.div(aa, PLANE)
    p = lax.rem(aa, PLANE)
    is_home = p >= HOME
    odd = lax.rem(p, 2) == 1
    has_plane = {d: (z >= -d) if d < 0 else (z < PLANES - d) for d in (-2, -1, 1, 2)}
    has_line = {d: (y >= -d) if d < 0 else (y < LINE - d) for d in (-2, -1, 1, 2)}
    sides = ((-2, 0, 0, 0), (2, 1, PLANE - ROWB, 1))
    in_far = {
        d: jnp.logical_and(p < ROWB if parity == 0 else p >= PLANE - ROWB, has_plane[d])
        for d, parity, _, _ in sides
    }
    home_far = {
        d: jnp.logical_and(jnp.logical_and(is_home, odd if parity else jnp.logical_not(odd)), has_plane[-d])
        for d, parity, _, _ in sides
    }

    def far_tiles(q, skip):
        return [(k, TILES * q + k - skip) for k in range(TILES) if 0 <= TILES * q + k - skip < BTILES]

    def at(d, q):
        return {"aa": aa + (d * PLANE - p) + q, "ba": y}

    def along(d):
        return {"aa": aa, "ba": y + d}

    loads = [pltpu.make_async_copy(this_hbm, xv, load_sem.at[0])]
    loads[0].start()

    barrier = pltpu.get_barrier_semaphore()

    def greet(to):
        pl.semaphore_signal(barrier, inc=1, device_id=to, device_id_type=MESH)

    for d in (-2, -1, 1, 2):

        @pl.when(has_line[d])
        def _(d=d):
            greet(along(d))

    for d in (-1, 1):

        @pl.when(has_plane[d])
        def _(d=d):
            for q in range(PLANE):
                greet(at(d, q))

    for q in range(1, PLANE):
        greet(at(0, lax.rem(p + q, PLANE)))

    for d, parity, low, _ in sides:

        @pl.when(in_far[d])
        def _(d=d, parity=parity):
            for cb in range(parity, COLB, 2):
                greet(at(d, HOME + cb))

        @pl.when(home_far[d])
        def _(d=d, low=low):
            for q in range(ROWB):
                greet(at(-d, low + q))

    loads += [
        pltpu.make_async_copy(diag_hbm, dv, load_sem.at[1]),
        pltpu.make_async_copy(prev_hbm, pv, load_sem.at[2]),
        pltpu.make_async_copy(bblk_hbm.at[pl.ds(y * COLB, COLB)], braw, load_sem.at[3]),
    ]
    blocks = PLANES * ROWB
    a_block = [lax.rem(z * ROWB - ROWB + j + blocks, blocks) for j in range(WIN - 1)]
    a_block.append(lax.rem(z * ROWB + jnp.where(odd, blocks - 4, 2 * ROWB), blocks))
    for k, (j, count) in enumerate(((0, ROWB), (ROWB, ROWB), (2 * ROWB, ROWB), (3 * ROWB, 1))):
        loads.append(
            pltpu.make_async_copy(
                ablk_hbm.at[pl.ds(a_block[j], count)], araw.at[pl.ds(j, count)], load_sem.at[4 + k]
            )
        )

    for c in loads[1:]:
        c.start()

    loads[0].wait()
    for cb in range(COLB):
        own = xv[:, cb * BLK : (cb + 1) * BLK].astype(jnp.bfloat16).reshape(TILES, TILE, BLK)
        xb[cb] = own
        for k, (tile, tiles) in enumerate(PARTS):
            yw0[k][9 + cb] = own[tile : tile + tiles]

    b_table = class_table(bcls)
    b_at = []
    for r in range(COLB):
        block = y * COLB + r
        start, length = class_of(block, b_table)
        b_at.append(
            [
                jnp.clip(
                    column_of(start, length, boff[k, block], 4) - y * COLB + 9, 0, YWIN - 1
                )
                for k in range(2)
            ]
        )
    greetings = PLANE - 1
    for d, _, _, _ in sides:
        greetings = greetings + jnp.where(in_far[d], COLB // 2, 0) + jnp.where(home_far[d], ROWB, 0)
    for d in (-2, -1, 1, 2):
        greetings = greetings + jnp.where(has_line[d], 1, 0)
    for d in (-1, 1):
        greetings = greetings + jnp.where(has_plane[d], PLANE, 0)
    pl.semaphore_wait(barrier, greetings)

    def y_copy(w, at_sem, k):
        src, n, dst, d = ((9, 6, 3, 1), (9, 6, 15, -1), (12, 3, 0, 2), (9, 3, 21, -2))[k]
        return d, remote(
            w.at[pl.ds(src, n)], w.at[pl.ds(dst, n)],
            y_sem.at[at_sem, 0, k], y_sem.at[at_sem, 1, k], along(d),
        )

    def y_start(w, at_sem):
        for k in range(4):
            d, copy = y_copy(w, at_sem, k)
            pl.when(has_line[d])(copy.start)

    def y_sent(w, at_sem):
        for k in range(4):
            d, copy = y_copy(w, at_sem, k)
            pl.when(has_line[d])(copy.wait_send)

    def y_arrived(w, at_sem):
        for k in range(4):
            d, copy = y_copy(w, at_sem, k)
            pl.when(has_line[-d])(copy.wait_recv)

    def piece(k):
        return pl.ds(TILES * k, TILES)

    def send_in(src, w, step, tile, tiles):
        def place(k):
            return w.at[pl.ds(TILES * k + tile, tiles)]

        for d, parity, low, skip in sides:
            for q in range(ROWB):
                spots = [(k, spot) for k, spot in far_tiles(q, skip) if tile <= k < tile + tiles]
                if spots:

                    @pl.when(jnp.logical_and(p == low + q, has_plane[d]))
                    def _(d=d, parity=parity, spots=spots):
                        for cb in range(parity, COLB, 2):
                            remote(
                                src.at[cb, pl.ds(spots[0][0] - tile, len(spots))],
                                w.at[pl.ds(FAR + spots[0][1], len(spots))],
                                in_send.at[step, 3], in_recv.at[step, 3], at(d, HOME + cb),
                            ).start()

        for k, d, base in ((2, -1, 2 * PLANE), (0, 1, 0)):

            @pl.when(has_plane[d])
            def _(k=k, d=d, base=base):
                for cb in range(COLB):
                    remote(
                        src.at[cb], place(base + p),
                        in_send.at[step, k], in_recv.at[step, k], at(d, HOME + cb),
                    ).start()

        def to_own(cb):
            remote(
                src.at[cb], place(PLANE + p),
                in_send.at[step, 1], in_recv.at[step, 1], at(0, HOME + cb),
            ).start()

        @pl.when(is_home)
        def _():
            for k in range(1, COLB):
                to_own(lax.rem(p - HOME + k, COLB))
            pltpu.make_async_copy(src.at[p - HOME], place(PLANE + p), self_sem.at[step]).start()

        @pl.when(jnp.logical_not(is_home))
        def _():
            for cb in range(COLB):
                to_own(cb)

    def await_pieces(count, sem):
        await_bytes(win0.at[pl.ds(0, count * TILES)], sem)

    def await_far_rows(sem):
        for d, _, low, skip in sides:
            for q in range(ROWB):
                count = COLB // 2 * len(far_tiles(q, skip))

                @pl.when(jnp.logical_and(p == low + q, has_plane[d]))
                def _(count=count):
                    await_bytes(win0.at[pl.ds(0, count)], sem)

    def await_far_block(sem):
        for d, _, _, _ in sides:
            pl.when(home_far[d])(lambda: await_bytes(win0.at[pl.ds(0, BTILES)], sem))

    def sent_in(step):
        await_far_rows(in_send.at[step, 3])
        pl.when(has_plane[-1])(lambda: await_pieces(COLB, in_send.at[step, 2]))
        pl.when(has_plane[1])(lambda: await_pieces(COLB, in_send.at[step, 0]))
        pl.when(is_home)(lambda: await_pieces(COLB - 1, in_send.at[step, 1]))
        pl.when(jnp.logical_not(is_home))(lambda: await_pieces(COLB, in_send.at[step, 1]))

    def arrived_in(step):
        await_pieces(1, self_sem.at[step])
        await_pieces(PLANE - 1, in_recv.at[step, 1])
        pl.when(has_plane[-1])(lambda: await_pieces(PLANE, in_recv.at[step, 0]))
        pl.when(has_plane[1])(lambda: await_pieces(PLANE, in_recv.at[step, 2]))
        await_far_block(in_recv.at[step, 3])

    def send_far(src, rec, step):
        for d, _, low, skip in sides:

            @pl.when(home_far[d])
            def _(d=d, low=low, skip=skip):
                for q in range(ROWB):
                    spots = far_tiles(q, skip)
                    remote(
                        src.at[pl.ds(FAR + spots[0][1], len(spots))],
                        rec.at[3, p - HOME, pl.ds(spots[0][0], len(spots))],
                        out_send.at[step, 3], out_recv.at[step, 3], at(-d, low + q),
                    ).start()

    def send_out(src, rec, step, d, base, slot):
        @pl.when(has_plane[d])
        def _():
            for q in range(PLANE):
                remote(
                    src.at[piece(base + q)], rec.at[slot, p - HOME],
                    out_send.at[step, slot], out_recv.at[step, slot], at(d, q),
                ).start()

    def send_own(src, rec, step):
        for k in range(1, PLANE):
            q = lax.rem(p + k, PLANE)
            remote(
                src.at[piece(PLANE + q)], rec.at[1, p - HOME],
                out_send.at[step, 1], out_recv.at[step, 1], at(0, q),
            ).start()
        pltpu.make_async_copy(
            src.at[piece(PLANE + p)], rec.at[1, p - HOME], self_sem.at[2 + step]
        ).start()

    def sent_out(step):
        await_pieces(PLANE - 1, out_send.at[step, 1])
        await_far_block(out_send.at[step, 3])
        pl.when(has_plane[1])(lambda: await_pieces(PLANE, out_send.at[step, 0]))
        pl.when(has_plane[-1])(lambda: await_pieces(PLANE, out_send.at[step, 2]))

    def arrived_out(step):
        await_far_rows(out_recv.at[step, 3])
        pl.when(has_plane[-1])(lambda: await_pieces(COLB, out_recv.at[step, 0]))
        pl.when(has_plane[1])(lambda: await_pieces(COLB, out_recv.at[step, 2]))
        pl.when(jnp.logical_not(is_home))(lambda: await_pieces(COLB, out_recv.at[step, 1]))

        @pl.when(is_home)
        def _():
            await_pieces(COLB - 1, out_recv.at[step, 1])
            await_pieces(1, self_sem.at[2 + step])

    for k in range(len(PARTS)):
        y_start(yw0[k], k)
    send_in(xb, win0, 0, 0, TILES)

    for c in loads[1:4]:
        c.wait()
    for r in range(COLB):
        for k in range(2):
            live = jnp.full((BLK, BLK), bmask[k, y * COLB + r].astype(jnp.float32))
            bw[r, :, k * BLK : (k + 1) * BLK] = braw[r, k] * live.astype(jnp.bfloat16)

    def beta(w, r, rows):
        both = jnp.concatenate([w[b_at[r][k]].reshape(rows, BLK) for k in range(2)], axis=1)
        return lax.dot_general(
            both, bw[r], (((1,), (1,)), ((), ())), preferred_element_type=jnp.float32
        )

    def couple(w, j):
        both = jnp.concatenate(
            [w[pl.ds(a_at[j][k] * 8, 8)].reshape(BLK, BLK) for k in range(2)], axis=0
        )
        return jnp.dot(aw[j], both, preferred_element_type=jnp.float32)

    def alpha(w, out, rows, more):
        for j in rows:
            product = couple(w, j)
            if more:
                product = product + pre[j]
            out[8 * j : 8 * (j + 1)] = product.astype(jnp.bfloat16).reshape(8, TILE, BLK)

    def alpha_and_send(w, out, rec, step, more):
        alpha(w, out, range(9, 10), more)
        send_far(out, rec, step)
        alpha(w, out, range(6, 9), more)
        send_out(out, rec, step, 1, 2 * PLANE, 0)
        alpha(w, out, range(0, 3), more)
        send_out(out, rec, step, -1, 0, 2)
        alpha(w, out, range(3, 6), more)
        send_own(out, rec, step)

    def send_all(out, rec, step):
        send_far(out, rec, step)
        send_out(out, rec, step, 1, 2 * PLANE, 0)
        send_out(out, rec, step, -1, 0, 2)
        send_own(out, rec, step)

    def returned(rec, cb):
        return jnp.concatenate(
            [rec[slot_at[cb % 2][q], cb, q] for q in range(TILES)], axis=0
        ).astype(jnp.float32)

    for k, (tile, tiles) in enumerate(PARTS):
        rows = slice(TILE * tile, TILE * (tile + tiles))
        y_arrived(yw0[k], k)
        for cb in range(COLB):
            cols = slice(cb * BLK, (cb + 1) * BLK)
            b1 = beta(yw0[k], cb, TILE * tiles).astype(jnp.bfloat16).astype(jnp.float32)
            t = 2.0 * (b1 + dv[rows, cols] * xv[rows, cols]) - pv[rows, cols]
            tv[rows, cols] = t
            yw1[9 + cb, tile : tile + tiles] = t.astype(jnp.bfloat16).reshape(tiles, TILE, BLK)
            tb[k][cb] = (t + 2.0 * b1).astype(jnp.bfloat16).reshape(tiles, TILE, BLK)
        send_in(tb[k], wint, 1, tile, tiles)
    y_start(yw1, len(PARTS))

    a_table = class_table(acls)
    a_at = []
    for j in range(WIN):
        start, length = class_of(a_block[j], a_table)
        spots = []
        for k in range(2):
            spot = column_of(start, length, aoff[k, a_block[j]], 3) - (z - 1) * ROWB
            spots.append(jnp.where(spot < 0, WIN - 1, jnp.minimum(spot, WIN - 1)))
        a_at.append(spots)
    slot_at = []
    for parity in range(2):
        slots = []
        for q in range(TILES):
            start, length = class_of(z * ROWB + lax.div(TILES * p + q, PLANE), a_table)
            away = lax.div(start + lax.div(length - 1 + parity, 2), ROWB) - z
            slot = jnp.where(jnp.logical_or(away < -1, away > 1), 3, away + 1)
            slots.append(jnp.clip(slot, 0, 3))
        slot_at.append(slots)

    for c in loads[4:]:
        c.wait()

    @pl.when(is_home)
    def _():
        for j in range(WIN):
            for k in range(2):
                live = jnp.full((BLK, BLK), amask[k, a_block[j]].astype(jnp.float32))
                aw[j, :, k * BLK : (k + 1) * BLK] = araw[j, k] * live.astype(jnp.bfloat16)


    @pl.when(is_home)
    def _():
        arrived_in(0)
        alpha(win0, al0, range(WIN), False)
        for j in range(WIN):
            pre[j] = 2.0 * couple(al0, j)
        send_all(al0, rec0, 0)
        arrived_in(1)
        alpha_and_send(wint, al1, rec1, 1, True)

    arrived_out(0)
    for cb in range(COLB):
        cols = slice(cb * BLK, (cb + 1) * BLK)
        nv[:, cols] = 2.0 * returned(rec0, cb) + tv[:, cols]
    y_arrived(yw1, len(PARTS))
    for cb in range(COLB):
        cols = slice(cb * BLK, (cb + 1) * BLK)
        tv[:, cols] = 2.0 * (beta(yw1, cb, ROWS) + dv[:, cols] * nv[:, cols]) - xv[:, cols]
    arrived_out(1)
    for cb in range(COLB):
        cols = slice(cb * BLK, (cb + 1) * BLK)
        ov[:, cols] = tv[:, cols] + 2.0 * returned(rec1, cb)

    for step in range(2):
        sent_in(step)
        pl.when(is_home)(lambda step=step: sent_out(step))
    for k in range(len(PARTS)):
        y_sent(yw0[k], k)
    y_sent(yw1, len(PARTS))


def hand_over(next_in, after_in, next_out, after_out, sem):
    copies = [
        pltpu.make_async_copy(next_in, next_out, sem.at[0]),
        pltpu.make_async_copy(after_in, after_out, sem.at[1]),
    ]
    for c in copies:
        c.start()
    for c in copies:
        c.wait()


def on_device(prev, this, diag, ablk, acls, aoff, amask, bblk, bcls, boff, bmask):
    rows, columns = ROWS, COLB * BLK
    f32, bf16 = jnp.float32, jnp.bfloat16
    hbm = pl.BlockSpec(memory_space=pltpu.HBM)
    vmem = pl.BlockSpec(memory_space=pltpu.VMEM)
    smem = pl.BlockSpec(memory_space=pltpu.SMEM)
    dma = pltpu.SemaphoreType.DMA
    next_vector, after_vector = pl.pallas_call(
        kernel,
        out_shape=[pltpu.VMEM((rows, columns), f32)] * 2,
        in_specs=[hbm, hbm, hbm, hbm, smem, smem, smem, hbm, smem, smem, smem],
        out_specs=[vmem, vmem],
        scratch_shapes=[
            *[pltpu.VMEM((rows, columns), f32)] * 4,
            pltpu.VMEM((COLB, TILES, TILE, BLK), bf16),
            pltpu.VMEM((YWIN, TILES, TILE, BLK), bf16),
            pltpu.VMEM((WIN, BLK, BLK), f32),
            *[pltpu.VMEM((WIN * BTILES, TILE, BLK), bf16)] * 4,
            *[pltpu.VMEM((4, COLB, TILES, TILE, BLK), bf16)] * 2,
            pltpu.VMEM((WIN, 2, BLK, BLK), bf16),
            pltpu.VMEM((COLB, 2, BLK, BLK), bf16),
            pltpu.VMEM((WIN, BLK, 2 * BLK), bf16),
            pltpu.VMEM((COLB, BLK, 2 * BLK), bf16),
            dma((8,)),
            *[dma((2, 4))] * 4,
            dma((1 + len(PARTS), 2, 4)),
            dma((4,)),
            *[pltpu.VMEM((YWIN, tiles, TILE, BLK), bf16) for _, tiles in PARTS],
            *[pltpu.VMEM((COLB, tiles, TILE, BLK), bf16) for _, tiles in PARTS],
        ],
        compiler_params=pltpu.CompilerParams(
            collective_id=0, has_side_effects=True, vmem_limit_bytes=60 * 1024 * 1024
        ),
        name="chebyshev_steps",
    )(prev, this, diag, ablk, acls, aoff.T, amask.T, bblk, bcls, boff.T, bmask.T)
    return pl.pallas_call(
        hand_over,
        out_shape=[jax.ShapeDtypeStruct((rows, columns), f32)] * 2,
        in_specs=[pl.BlockSpec(memory_space=pl.ANY)] * 2,
        out_specs=[hbm, hbm],
        scratch_shapes=[dma((2,))],
        compiler_params=pltpu.CompilerParams(vmem_limit_bytes=1024 * 1024),
        name="hand_over",
    )(next_vector, after_vector)


def solution(mesh):
    own = P("aa", "ba")
    return jax.shard_map(
        on_device,
        mesh=mesh,
        in_specs=(own, own, own, *[P()] * 8),
        out_specs=(own, own),
        check_vma=False,
    )
```

```python
import jax
import jax.numpy as jnp
from jax import lax
from jax.experimental import pallas as pl
from jax.experimental.pallas import tpu as pltpu
from jax.sharding import PartitionSpec as P

BLK = 128
PLANES = 12
PLANE = 8
LINE = 8
ROWS = 48
COLB = 6
HOME = 2
ROWB = 3
WIN = 10
TILE = 16
TILES = 3
PARTS = ((0, 1), (1, 1), (2, 1))
BTILES = 8
FAR = 72
YWIN = 24
NCLS = 8
MESH = pl.DeviceIdType.MESH


def remote(src, dst, send, recv, to):
    return pltpu.make_async_remote_copy(
        src_ref=src, dst_ref=dst, send_sem=send, recv_sem=recv, device_id=to, device_id_type=MESH
    )


def await_bytes(ref, sem):
    pltpu.make_async_copy(ref, ref, sem).wait()


def class_table(sizes):
    starts, lengths, first = [], [], jnp.int32(0)
    for c in range(NCLS):
        starts.append(first)
        lengths.append(sizes[c])
        first = first + sizes[c]
    return starts, lengths


def class_of(block, table):
    starts, lengths = table
    start, length = starts[0], lengths[0]
    for c in range(1, NCLS):
        later = block >= starts[c]
        start = jnp.where(later, starts[c], start)
        length = jnp.where(later, lengths[c], length)
    return start, length


def column_of(start, length, offset, halvings):
    for k in reversed(range(halvings)):
        step = length * (1 << k)
        offset = jnp.where(offset >= step, offset - step, offset)
    return start + offset


def kernel(
    prev_hbm, this_hbm, diag_hbm, ablk_hbm, acls, aoff, amask, bblk_hbm, bcls, boff, bmask,
    nv, ov,
    xv, pv, dv, tv, xb, yw1, pre, win0, wint, al0, al1, rec0, rec1, araw, braw, aw, bw,
    load_sem, in_send, in_recv, out_send, out_recv, y_sem, self_sem, *parts,
):
    yw0, tb = parts[: len(PARTS)], parts[len(PARTS) :]
    aa = lax.axis_index("aa")
    y = lax.axis_index("ba")
    z = lax.div(aa, PLANE)
    p = lax.rem(aa, PLANE)
    is_home = p >= HOME
    odd = lax.rem(p, 2) == 1
    has_plane = {d: (z >= -d) if d < 0 else (z < PLANES - d) for d in (-2, -1, 1, 2)}
    has_line = {d: (y >= -d) if d < 0 else (y < LINE - d) for d in (-2, -1, 1, 2)}
    sides = ((-2, 0, 0, 0), (2, 1, PLANE - ROWB, 1))
    in_far = {
        d: jnp.logical_and(p < ROWB if parity == 0 else p >= PLANE - ROWB, has_plane[d])
        for d, parity, _, _ in sides
    }
    home_far = {
        d: jnp.logical_and(jnp.logical_and(is_home, odd if parity else jnp.logical_not(odd)), has_plane[-d])
        for d, parity, _, _ in sides
    }

    def far_tiles(q, skip):
        return [(k, TILES * q + k - skip) for k in range(TILES) if 0 <= TILES * q + k - skip < BTILES]

    def at(d, q):
        return {"aa": aa + (d * PLANE - p) + q, "ba": y}

    def along(d):
        return {"aa": aa, "ba": y + d}

    loads = [pltpu.make_async_copy(this_hbm, xv, load_sem.at[0])]
    loads[0].start()

    barrier = pltpu.get_barrier_semaphore()

    def greet(to):
        pl.semaphore_signal(barrier, inc=1, device_id=to, device_id_type=MESH)

    for d in (-2, -1, 1, 2):

        @pl.when(has_line[d])
        def _(d=d):
            greet(along(d))

    for d in (-1, 1):

        @pl.when(has_plane[d])
        def _(d=d):
            for q in range(PLANE):
                greet(at(d, q))

    for q in range(1, PLANE):
        greet(at(0, lax.rem(p + q, PLANE)))

    for d, parity, low, _ in sides:

        @pl.when(in_far[d])
        def _(d=d, parity=parity):
            for cb in range(parity, COLB, 2):
                greet(at(d, HOME + cb))

        @pl.when(home_far[d])
        def _(d=d, low=low):
            for q in range(ROWB):
                greet(at(-d, low + q))

    loads += [
        pltpu.make_async_copy(diag_hbm, dv, load_sem.at[1]),
        pltpu.make_async_copy(prev_hbm, pv, load_sem.at[2]),
        pltpu.make_async_copy(bblk_hbm.at[pl.ds(y * COLB, COLB)], braw, load_sem.at[3]),
    ]
    blocks = PLANES * ROWB
    a_block = [lax.rem(z * ROWB - ROWB + j + blocks, blocks) for j in range(WIN - 1)]
    a_block.append(lax.rem(z * ROWB + jnp.where(odd, blocks - 4, 2 * ROWB), blocks))
    for k, (j, count) in enumerate(((0, ROWB), (ROWB, ROWB), (2 * ROWB, ROWB), (3 * ROWB, 1))):
        loads.append(
            pltpu.make_async_copy(
                ablk_hbm.at[pl.ds(a_block[j], count)], araw.at[pl.ds(j, count)], load_sem.at[4 + k]
            )
        )

    for c in loads[1:]:
        c.start()

    loads[0].wait()
    for cb in range(COLB):
        own = xv[:, cb * BLK : (cb + 1) * BLK].astype(jnp.bfloat16).reshape(TILES, TILE, BLK)
        xb[cb] = own
        for k, (tile, tiles) in enumerate(PARTS):
            yw0[k][9 + cb] = own[tile : tile + tiles]

    b_table = class_table(bcls)
    b_at = []
    for r in range(COLB):
        block = y * COLB + r
        start, length = class_of(block, b_table)
        b_at.append(
            [
                jnp.clip(
                    column_of(start, length, boff[k, block], 4) - y * COLB + 9, 0, YWIN - 1
                )
                for k in range(2)
            ]
        )
    greetings = PLANE - 1
    for d, _, _, _ in sides:
        greetings = greetings + jnp.where(in_far[d], COLB // 2, 0) + jnp.where(home_far[d], ROWB, 0)
    for d in (-2, -1, 1, 2):
        greetings = greetings + jnp.where(has_line[d], 1, 0)
    for d in (-1, 1):
        greetings = greetings + jnp.where(has_plane[d], PLANE, 0)
    pl.semaphore_wait(barrier, greetings)

    def y_copy(w, at_sem, k):
        src, n, dst, d = ((9, 6, 3, 1), (9, 6, 15, -1), (12, 3, 0, 2), (9, 3, 21, -2))[k]
        return d, remote(
            w.at[pl.ds(src, n)], w.at[pl.ds(dst, n)],
            y_sem.at[at_sem, 0, k], y_sem.at[at_sem, 1, k], along(d),
        )

    def y_start(w, at_sem):
        for k in range(4):
            d, copy = y_copy(w, at_sem, k)
            pl.when(has_line[d])(copy.start)

    def y_sent(w, at_sem):
        for k in range(4):
            d, copy = y_copy(w, at_sem, k)
            pl.when(has_line[d])(copy.wait_send)

    def y_arrived(w, at_sem):
        for k in range(4):
            d, copy = y_copy(w, at_sem, k)
            pl.when(has_line[-d])(copy.wait_recv)

    def piece(k):
        return pl.ds(TILES * k, TILES)

    def send_in(src, w, step, tile, tiles):
        def place(k):
            return w.at[pl.ds(TILES * k + tile, tiles)]

        for d, parity, low, skip in sides:
            for q in range(ROWB):
                spots = [(k, spot) for k, spot in far_tiles(q, skip) if tile <= k < tile + tiles]
                if spots:

                    @pl.when(jnp.logical_and(p == low + q, has_plane[d]))
                    def _(d=d, parity=parity, spots=spots):
                        for cb in range(parity, COLB, 2):
                            remote(
                                src.at[cb, pl.ds(spots[0][0] - tile, len(spots))],
                                w.at[pl.ds(FAR + spots[0][1], len(spots))],
                                in_send.at[step, 3], in_recv.at[step, 3], at(d, HOME + cb),
                            ).start()

        for k, d, base in ((2, -1, 2 * PLANE), (0, 1, 0)):

            @pl.when(has_plane[d])
            def _(k=k, d=d, base=base):
                for cb in range(COLB):
                    remote(
                        src.at[cb], place(base + p),
                        in_send.at[step, k], in_recv.at[step, k], at(d, HOME + cb),
                    ).start()

        def to_own(cb):
            remote(
                src.at[cb], place(PLANE + p),
                in_send.at[step, 1], in_recv.at[step, 1], at(0, HOME + cb),
            ).start()

        @pl.when(is_home)
        def _():
            for k in range(1, COLB):
                to_own(lax.rem(p - HOME + k, COLB))
            pltpu.make_async_copy(src.at[p - HOME], place(PLANE + p), self_sem.at[step]).start()

        @pl.when(jnp.logical_not(is_home))
        def _():
            for cb in range(COLB):
                to_own(cb)

    def await_pieces(count, sem):
        await_bytes(win0.at[pl.ds(0, count * TILES)], sem)

    def await_far_rows(sem):
        for d, _, low, skip in sides:
            for q in range(ROWB):
                count = COLB // 2 * len(far_tiles(q, skip))

                @pl.when(jnp.logical_and(p == low + q, has_plane[d]))
                def _(count=count):
                    await_bytes(win0.at[pl.ds(0, count)], sem)

    def await_far_block(sem):
        for d, _, _, _ in sides:
            pl.when(home_far[d])(lambda: await_bytes(win0.at[pl.ds(0, BTILES)], sem))

    def sent_in(step):
        await_far_rows(in_send.at[step, 3])
        pl.when(has_plane[-1])(lambda: await_pieces(COLB, in_send.at[step, 2]))
        pl.when(has_plane[1])(lambda: await_pieces(COLB, in_send.at[step, 0]))
        pl.when(is_home)(lambda: await_pieces(COLB - 1, in_send.at[step, 1]))
        pl.when(jnp.logical_not(is_home))(lambda: await_pieces(COLB, in_send.at[step, 1]))

    def arrived_in(step):
        await_pieces(1, self_sem.at[step])
        await_pieces(PLANE - 1, in_recv.at[step, 1])
        pl.when(has_plane[-1])(lambda: await_pieces(PLANE, in_recv.at[step, 0]))
        pl.when(has_plane[1])(lambda: await_pieces(PLANE, in_recv.at[step, 2]))
        await_far_block(in_recv.at[step, 3])

    def send_far(src, rec, step):
        for d, _, low, skip in sides:

            @pl.when(home_far[d])
            def _(d=d, low=low, skip=skip):
                for q in range(ROWB):
                    spots = far_tiles(q, skip)
                    remote(
                        src.at[pl.ds(FAR + spots[0][1], len(spots))],
                        rec.at[3, p - HOME, pl.ds(spots[0][0], len(spots))],
                        out_send.at[step, 3], out_recv.at[step, 3], at(-d, low + q),
                    ).start()

    def send_out(src, rec, step, d, base, slot):
        @pl.when(has_plane[d])
        def _():
            for q in range(PLANE):
                remote(
                    src.at[piece(base + q)], rec.at[slot, p - HOME],
                    out_send.at[step, slot], out_recv.at[step, slot], at(d, q),
                ).start()

    def send_own(src, rec, step):
        for k in range(1, PLANE):
            q = lax.rem(p + k, PLANE)
            remote(
                src.at[piece(PLANE + q)], rec.at[1, p - HOME],
                out_send.at[step, 1], out_recv.at[step, 1], at(0, q),
            ).start()
        pltpu.make_async_copy(
            src.at[piece(PLANE + p)], rec.at[1, p - HOME], self_sem.at[2 + step]
        ).start()

    def sent_out(step):
        await_pieces(PLANE - 1, out_send.at[step, 1])
        await_far_block(out_send.at[step, 3])
        pl.when(has_plane[1])(lambda: await_pieces(PLANE, out_send.at[step, 0]))
        pl.when(has_plane[-1])(lambda: await_pieces(PLANE, out_send.at[step, 2]))

    def arrived_out(step):
        await_far_rows(out_recv.at[step, 3])
        pl.when(has_plane[-1])(lambda: await_pieces(COLB, out_recv.at[step, 0]))
        pl.when(has_plane[1])(lambda: await_pieces(COLB, out_recv.at[step, 2]))
        pl.when(jnp.logical_not(is_home))(lambda: await_pieces(COLB, out_recv.at[step, 1]))

        @pl.when(is_home)
        def _():
            await_pieces(COLB - 1, out_recv.at[step, 1])
            await_pieces(1, self_sem.at[2 + step])

    for k in range(len(PARTS)):
        y_start(yw0[k], k)
    send_in(xb, win0, 0, 0, TILES)

    for c in loads[1:4]:
        c.wait()
    for r in range(COLB):
        for k in range(2):
            live = jnp.full((BLK, BLK), bmask[k, y * COLB + r].astype(jnp.float32))
            bw[r, :, k * BLK : (k + 1) * BLK] = braw[r, k] * live.astype(jnp.bfloat16)

    def beta(w, r, rows):
        both = jnp.concatenate([w[b_at[r][k]].reshape(rows, BLK) for k in range(2)], axis=1)
        return lax.dot_general(
            both, bw[r], (((1,), (1,)), ((), ())), preferred_element_type=jnp.float32
        )

    def couple(w, j):
        both = jnp.concatenate(
            [w[pl.ds(a_at[j][k] * 8, 8)].reshape(BLK, BLK) for k in range(2)], axis=0
        )
        return jnp.dot(aw[j], both, preferred_element_type=jnp.float32)

    def alpha(w, out, rows, more):
        for j in rows:
            product = couple(w, j)
            if more:
                product = product + pre[j]
            out[8 * j : 8 * (j + 1)] = product.astype(jnp.bfloat16).reshape(8, TILE, BLK)

    def alpha_and_send(w, out, rec, step, more):
        alpha(w, out, range(9, 10), more)
        send_far(out, rec, step)
        alpha(w, out, range(6, 9), more)
        send_out(out, rec, step, 1, 2 * PLANE, 0)
        alpha(w, out, range(0, 3), more)
        send_out(out, rec, step, -1, 0, 2)
        alpha(w, out, range(3, 6), more)
        send_own(out, rec, step)

    def send_all(out, rec, step):
        send_far(out, rec, step)
        send_out(out, rec, step, 1, 2 * PLANE, 0)
        send_out(out, rec, step, -1, 0, 2)
        send_own(out, rec, step)

    def returned(rec, cb):
        return jnp.concatenate(
            [rec[slot_at[cb % 2][q], cb, q] for q in range(TILES)], axis=0
        ).astype(jnp.float32)

    for k, (tile, tiles) in enumerate(PARTS):
        rows = slice(TILE * tile, TILE * (tile + tiles))
        y_arrived(yw0[k], k)
        for cb in range(COLB):
            cols = slice(cb * BLK, (cb + 1) * BLK)
            b1 = beta(yw0[k], cb, TILE * tiles).astype(jnp.bfloat16).astype(jnp.float32)
            t = 2.0 * (b1 + dv[rows, cols] * xv[rows, cols]) - pv[rows, cols]
            tv[rows, cols] = t
            yw1[9 + cb, tile : tile + tiles] = t.astype(jnp.bfloat16).reshape(tiles, TILE, BLK)
            tb[k][cb] = (t + 2.0 * b1).astype(jnp.bfloat16).reshape(tiles, TILE, BLK)
        send_in(tb[k], wint, 1, tile, tiles)
    y_start(yw1, len(PARTS))

    a_table = class_table(acls)
    a_at = []
    for j in range(WIN):
        start, length = class_of(a_block[j], a_table)
        spots = []
        for k in range(2):
            spot = column_of(start, length, aoff[k, a_block[j]], 3) - (z - 1) * ROWB
            spots.append(jnp.where(spot < 0, WIN - 1, jnp.minimum(spot, WIN - 1)))
        a_at.append(spots)
    slot_at = []
    for parity in range(2):
        slots = []
        for q in range(TILES):
            start, length = class_of(z * ROWB + lax.div(TILES * p + q, PLANE), a_table)
            away = lax.div(start + lax.div(length - 1 + parity, 2), ROWB) - z
            slot = jnp.where(jnp.logical_or(away < -1, away > 1), 3, away + 1)
            slots.append(jnp.clip(slot, 0, 3))
        slot_at.append(slots)

    for c in loads[4:]:
        c.wait()

    @pl.when(is_home)
    def _():
        for j in range(WIN):
            for k in range(2):
                live = jnp.full((BLK, BLK), amask[k, a_block[j]].astype(jnp.float32))
                aw[j, :, k * BLK : (k + 1) * BLK] = araw[j, k] * live.astype(jnp.bfloat16)


    @pl.when(is_home)
    def _():
        arrived_in(0)
        alpha(win0, al0, range(WIN), False)
        for j in range(WIN):
            pre[j] = 2.0 * couple(al0, j)
        send_all(al0, rec0, 0)
        arrived_in(1)
        alpha_and_send(wint, al1, rec1, 1, True)

    arrived_out(0)
    for cb in range(COLB):
        cols = slice(cb * BLK, (cb + 1) * BLK)
        nv[:, cols] = 2.0 * returned(rec0, cb) + tv[:, cols]
    y_arrived(yw1, len(PARTS))
    for cb in range(COLB):
        cols = slice(cb * BLK, (cb + 1) * BLK)
        tv[:, cols] = 2.0 * (beta(yw1, cb, ROWS) + dv[:, cols] * nv[:, cols]) - xv[:, cols]
    for step in range(2):
        sent_in(step)
        pl.when(is_home)(lambda step=step: sent_out(step))
    for k in range(len(PARTS)):
        y_sent(yw0[k], k)
    y_sent(yw1, len(PARTS))
    arrived_out(1)
    for cb in range(COLB):
        cols = slice(cb * BLK, (cb + 1) * BLK)
        ov[:, cols] = tv[:, cols] + 2.0 * returned(rec1, cb)


def hand_over(next_in, after_in, next_out, after_out, sem):
    copies = [
        pltpu.make_async_copy(next_in, next_out, sem.at[0]),
        pltpu.make_async_copy(after_in, after_out, sem.at[1]),
    ]
    for c in copies:
        c.start()
    for c in copies:
        c.wait()


def on_device(prev, this, diag, ablk, acls, aoff, amask, bblk, bcls, boff, bmask):
    rows, columns = ROWS, COLB * BLK
    f32, bf16 = jnp.float32, jnp.bfloat16
    hbm = pl.BlockSpec(memory_space=pltpu.HBM)
    vmem = pl.BlockSpec(memory_space=pltpu.VMEM)
    smem = pl.BlockSpec(memory_space=pltpu.SMEM)
    dma = pltpu.SemaphoreType.DMA
    next_vector, after_vector = pl.pallas_call(
        kernel,
        out_shape=[pltpu.VMEM((rows, columns), f32)] * 2,
        in_specs=[hbm, hbm, hbm, hbm, smem, smem, smem, hbm, smem, smem, smem],
        out_specs=[vmem, vmem],
        scratch_shapes=[
            *[pltpu.VMEM((rows, columns), f32)] * 4,
            pltpu.VMEM((COLB, TILES, TILE, BLK), bf16),
            pltpu.VMEM((YWIN, TILES, TILE, BLK), bf16),
            pltpu.VMEM((WIN, BLK, BLK), f32),
            *[pltpu.VMEM((WIN * BTILES, TILE, BLK), bf16)] * 4,
            *[pltpu.VMEM((4, COLB, TILES, TILE, BLK), bf16)] * 2,
            pltpu.VMEM((WIN, 2, BLK, BLK), bf16),
            pltpu.VMEM((COLB, 2, BLK, BLK), bf16),
            pltpu.VMEM((WIN, BLK, 2 * BLK), bf16),
            pltpu.VMEM((COLB, BLK, 2 * BLK), bf16),
            dma((8,)),
            *[dma((2, 4))] * 4,
            dma((1 + len(PARTS), 2, 4)),
            dma((4,)),
            *[pltpu.VMEM((YWIN, tiles, TILE, BLK), bf16) for _, tiles in PARTS],
            *[pltpu.VMEM((COLB, tiles, TILE, BLK), bf16) for _, tiles in PARTS],
        ],
        compiler_params=pltpu.CompilerParams(
            collective_id=0, has_side_effects=True, vmem_limit_bytes=60 * 1024 * 1024
        ),
        name="chebyshev_steps",
    )(prev, this, diag, ablk, acls, aoff.T, amask.T, bblk, bcls, boff.T, bmask.T)
    return pl.pallas_call(
        hand_over,
        out_shape=[jax.ShapeDtypeStruct((rows, columns), f32)] * 2,
        in_specs=[pl.BlockSpec(memory_space=pl.ANY)] * 2,
        out_specs=[hbm, hbm],
        scratch_shapes=[dma((2,))],
        compiler_params=pltpu.CompilerParams(vmem_limit_bytes=1024 * 1024),
        name="hand_over",
    )(next_vector, after_vector)


def solution(mesh):
    own = P("aa", "ba")
    return jax.shard_map(
        on_device,
        mesh=mesh,
        in_specs=(own, own, own, *[P()] * 8),
        out_specs=(own, own),
        check_vma=False,
    )
```

```python
import jax
import jax.numpy as jnp
from jax import lax
from jax.experimental import pallas as pl
from jax.experimental.pallas import tpu as pltpu
from jax.sharding import PartitionSpec as P

BLK = 128
PLANES = 12
PLANE = 8
LINE = 8
ROWS = 48
COLB = 6
HOME = 2
ROWB = 3
WIN = 10
TILE = 16
TILES = 3
PARTS = ((0, 1), (1, 1), (2, 1))
BTILES = 8
FAR = 72
YWIN = 24
NCLS = 8
MESH = pl.DeviceIdType.MESH


def remote(src, dst, send, recv, to):
    return pltpu.make_async_remote_copy(
        src_ref=src, dst_ref=dst, send_sem=send, recv_sem=recv, device_id=to, device_id_type=MESH
    )


def await_bytes(ref, sem):
    pltpu.make_async_copy(ref, ref, sem).wait()


def class_table(sizes):
    starts, lengths, first = [], [], jnp.int32(0)
    for c in range(NCLS):
        starts.append(first)
        lengths.append(sizes[c])
        first = first + sizes[c]
    return starts, lengths


def class_of(block, table):
    starts, lengths = table
    start, length = starts[0], lengths[0]
    for c in range(1, NCLS):
        later = block >= starts[c]
        start = jnp.where(later, starts[c], start)
        length = jnp.where(later, lengths[c], length)
    return start, length


def column_of(start, length, offset, halvings):
    for k in reversed(range(halvings)):
        step = length * (1 << k)
        offset = jnp.where(offset >= step, offset - step, offset)
    return start + offset


def kernel(
    prev_hbm, this_hbm, diag_hbm, ablk_hbm, acls, aoff, amask, bblk_hbm, bcls, boff, bmask,
    nv, ov,
    xv, pv, dv, tv, xb, yw1, pre, win0, wint, al0, al1, rec0, rec1, araw, braw, aw, bw,
    load_sem, x_sem, in_send, in_recv, out_send, out_recv, y_sem, self_sem, *parts,
):
    yw0, tb = parts[: len(PARTS)], parts[len(PARTS) :]
    aa = lax.axis_index("aa")
    y = lax.axis_index("ba")
    z = lax.div(aa, PLANE)
    p = lax.rem(aa, PLANE)
    is_home = p >= HOME
    odd = lax.rem(p, 2) == 1
    has_plane = {d: (z >= -d) if d < 0 else (z < PLANES - d) for d in (-2, -1, 1, 2)}
    has_line = {d: (y >= -d) if d < 0 else (y < LINE - d) for d in (-2, -1, 1, 2)}
    sides = ((-2, 0, 0, 0), (2, 1, PLANE - ROWB, 1))
    in_far = {
        d: jnp.logical_and(p < ROWB if parity == 0 else p >= PLANE - ROWB, has_plane[d])
        for d, parity, _, _ in sides
    }
    home_far = {
        d: jnp.logical_and(jnp.logical_and(is_home, odd if parity else jnp.logical_not(odd)), has_plane[-d])
        for d, parity, _, _ in sides
    }

    def far_tiles(q, skip):
        return [(k, TILES * q + k - skip) for k in range(TILES) if 0 <= TILES * q + k - skip < BTILES]

    def at(d, q):
        return {"aa": aa + (d * PLANE - p) + q, "ba": y}

    def along(d):
        return {"aa": aa, "ba": y + d}

    x_loads = [
        pltpu.make_async_copy(
            this_hbm.at[pl.ds(TILE * k, TILE)], xv.at[pl.ds(TILE * k, TILE)], x_sem.at[k]
        )
        for k in range(TILES)
    ]
    for c in x_loads:
        c.start()

    barrier = pltpu.get_barrier_semaphore()

    def greet(to):
        pl.semaphore_signal(barrier, inc=1, device_id=to, device_id_type=MESH)

    for d in (-2, -1, 1, 2):

        @pl.when(has_line[d])
        def _(d=d):
            greet(along(d))

    for d in (-1, 1):

        @pl.when(has_plane[d])
        def _(d=d):
            for q in range(PLANE):
                greet(at(d, q))

    for q in range(1, PLANE):
        greet(at(0, lax.rem(p + q, PLANE)))

    for d, parity, low, _ in sides:

        @pl.when(in_far[d])
        def _(d=d, parity=parity):
            for cb in range(parity, COLB, 2):
                greet(at(d, HOME + cb))

        @pl.when(home_far[d])
        def _(d=d, low=low):
            for q in range(ROWB):
                greet(at(-d, low + q))

    loads = [
        pltpu.make_async_copy(diag_hbm, dv, load_sem.at[1]),
        pltpu.make_async_copy(prev_hbm, pv, load_sem.at[2]),
        pltpu.make_async_copy(bblk_hbm.at[pl.ds(y * COLB, COLB)], braw, load_sem.at[3]),
    ]
    blocks = PLANES * ROWB
    a_block = [lax.rem(z * ROWB - ROWB + j + blocks, blocks) for j in range(WIN - 1)]
    a_block.append(lax.rem(z * ROWB + jnp.where(odd, blocks - 4, 2 * ROWB), blocks))
    for k, (j, count) in enumerate(((0, ROWB), (ROWB, ROWB), (2 * ROWB, ROWB), (3 * ROWB, 1))):
        loads.append(
            pltpu.make_async_copy(
                ablk_hbm.at[pl.ds(a_block[j], count)], araw.at[pl.ds(j, count)], load_sem.at[4 + k]
            )
        )

    for c in loads:
        c.start()

    for c in x_loads:
        c.wait()
    for cb in range(COLB):
        own = xv[:, cb * BLK : (cb + 1) * BLK].astype(jnp.bfloat16).reshape(TILES, TILE, BLK)
        xb[cb] = own
        for k, (tile, tiles) in enumerate(PARTS):
            yw0[k][9 + cb] = own[tile : tile + tiles]

    b_table = class_table(bcls)
    b_at = []
    for r in range(COLB):
        block = y * COLB + r
        start, length = class_of(block, b_table)
        b_at.append(
            [
                jnp.clip(
                    column_of(start, length, boff[k, block], 4) - y * COLB + 9, 0, YWIN - 1
                )
                for k in range(2)
            ]
        )
    greetings = PLANE - 1
    for d, _, _, _ in sides:
        greetings = greetings + jnp.where(in_far[d], COLB // 2, 0) + jnp.where(home_far[d], ROWB, 0)
    for d in (-2, -1, 1, 2):
        greetings = greetings + jnp.where(has_line[d], 1, 0)
    for d in (-1, 1):
        greetings = greetings + jnp.where(has_plane[d], PLANE, 0)
    pl.semaphore_wait(barrier, greetings)

    def y_copy(w, at_sem, k):
        src, n, dst, d = ((9, 6, 3, 1), (9, 6, 15, -1), (12, 3, 0, 2), (9, 3, 21, -2))[k]
        return d, remote(
            w.at[pl.ds(src, n)], w.at[pl.ds(dst, n)],
            y_sem.at[at_sem, 0, k], y_sem.at[at_sem, 1, k], along(d),
        )

    def y_start(w, at_sem):
        for k in range(4):
            d, copy = y_copy(w, at_sem, k)
            pl.when(has_line[d])(copy.start)

    def y_sent(w, at_sem):
        for k in range(4):
            d, copy = y_copy(w, at_sem, k)
            pl.when(has_line[d])(copy.wait_send)

    def y_arrived(w, at_sem):
        for k in range(4):
            d, copy = y_copy(w, at_sem, k)
            pl.when(has_line[-d])(copy.wait_recv)

    def piece(k):
        return pl.ds(TILES * k, TILES)

    def send_in(src, w, step, tile, tiles):
        def place(k):
            return w.at[pl.ds(TILES * k + tile, tiles)]

        for d, parity, low, skip in sides:
            for q in range(ROWB):
                spots = [(k, spot) for k, spot in far_tiles(q, skip) if tile <= k < tile + tiles]
                if spots:

                    @pl.when(jnp.logical_and(p == low + q, has_plane[d]))
                    def _(d=d, parity=parity, spots=spots):
                        for cb in range(parity, COLB, 2):
                            remote(
                                src.at[cb, pl.ds(spots[0][0] - tile, len(spots))],
                                w.at[pl.ds(FAR + spots[0][1], len(spots))],
                                in_send.at[step, 3], in_recv.at[step, 3], at(d, HOME + cb),
                            ).start()

        for k, d, base in ((2, -1, 2 * PLANE), (0, 1, 0)):

            @pl.when(has_plane[d])
            def _(k=k, d=d, base=base):
                for cb in range(COLB):
                    remote(
                        src.at[cb], place(base + p),
                        in_send.at[step, k], in_recv.at[step, k], at(d, HOME + cb),
                    ).start()

        def to_own(cb):
            remote(
                src.at[cb], place(PLANE + p),
                in_send.at[step, 1], in_recv.at[step, 1], at(0, HOME + cb),
            ).start()

        @pl.when(is_home)
        def _():
            for k in range(1, COLB):
                to_own(lax.rem(p - HOME + k, COLB))
            pltpu.make_async_copy(src.at[p - HOME], place(PLANE + p), self_sem.at[step]).start()

        @pl.when(jnp.logical_not(is_home))
        def _():
            for cb in range(COLB):
                to_own(cb)

    def await_pieces(count, sem):
        await_bytes(win0.at[pl.ds(0, count * TILES)], sem)

    def await_far_rows(sem):
        for d, _, low, skip in sides:
            for q in range(ROWB):
                count = COLB // 2 * len(far_tiles(q, skip))

                @pl.when(jnp.logical_and(p == low + q, has_plane[d]))
                def _(count=count):
                    await_bytes(win0.at[pl.ds(0, count)], sem)

    def await_far_block(sem):
        for d, _, _, _ in sides:
            pl.when(home_far[d])(lambda: await_bytes(win0.at[pl.ds(0, BTILES)], sem))

    def sent_in(step):
        await_far_rows(in_send.at[step, 3])
        pl.when(has_plane[-1])(lambda: await_pieces(COLB, in_send.at[step, 2]))
        pl.when(has_plane[1])(lambda: await_pieces(COLB, in_send.at[step, 0]))
        pl.when(is_home)(lambda: await_pieces(COLB - 1, in_send.at[step, 1]))
        pl.when(jnp.logical_not(is_home))(lambda: await_pieces(COLB, in_send.at[step, 1]))

    def arrived_in(step):
        await_pieces(1, self_sem.at[step])
        await_pieces(PLANE - 1, in_recv.at[step, 1])
        pl.when(has_plane[-1])(lambda: await_pieces(PLANE, in_recv.at[step, 0]))
        pl.when(has_plane[1])(lambda: await_pieces(PLANE, in_recv.at[step, 2]))
        await_far_block(in_recv.at[step, 3])

    def send_far(src, rec, step):
        for d, _, low, skip in sides:

            @pl.when(home_far[d])
            def _(d=d, low=low, skip=skip):
                for q in range(ROWB):
                    spots = far_tiles(q, skip)
                    remote(
                        src.at[pl.ds(FAR + spots[0][1], len(spots))],
                        rec.at[3, p - HOME, pl.ds(spots[0][0], len(spots))],
                        out_send.at[step, 3], out_recv.at[step, 3], at(-d, low + q),
                    ).start()

    def send_out(src, rec, step, d, base, slot):
        @pl.when(has_plane[d])
        def _():
            for q in range(PLANE):
                remote(
                    src.at[piece(base + q)], rec.at[slot, p - HOME],
                    out_send.at[step, slot], out_recv.at[step, slot], at(d, q),
                ).start()

    def send_own(src, rec, step):
        for k in range(1, PLANE):
            q = lax.rem(p + k, PLANE)
            remote(
                src.at[piece(PLANE + q)], rec.at[1, p - HOME],
                out_send.at[step, 1], out_recv.at[step, 1], at(0, q),
            ).start()
        pltpu.make_async_copy(
            src.at[piece(PLANE + p)], rec.at[1, p - HOME], self_sem.at[2 + step]
        ).start()

    def sent_out(step):
        await_pieces(PLANE - 1, out_send.at[step, 1])
        await_far_block(out_send.at[step, 3])
        pl.when(has_plane[1])(lambda: await_pieces(PLANE, out_send.at[step, 0]))
        pl.when(has_plane[-1])(lambda: await_pieces(PLANE, out_send.at[step, 2]))

    def arrived_out(step):
        await_far_rows(out_recv.at[step, 3])
        pl.when(has_plane[-1])(lambda: await_pieces(COLB, out_recv.at[step, 0]))
        pl.when(has_plane[1])(lambda: await_pieces(COLB, out_recv.at[step, 2]))
        pl.when(jnp.logical_not(is_home))(lambda: await_pieces(COLB, out_recv.at[step, 1]))

        @pl.when(is_home)
        def _():
            await_pieces(COLB - 1, out_recv.at[step, 1])
            await_pieces(1, self_sem.at[2 + step])

    for k in range(len(PARTS)):
        y_start(yw0[k], k)
    send_in(xb, win0, 0, 0, TILES)

    for c in loads[:3]:
        c.wait()
    for r in range(COLB):
        for k in range(2):
            live = jnp.full((BLK, BLK), bmask[k, y * COLB + r].astype(jnp.float32))
            bw[r, :, k * BLK : (k + 1) * BLK] = braw[r, k] * live.astype(jnp.bfloat16)

    def beta(w, r, rows):
        both = jnp.concatenate([w[b_at[r][k]].reshape(rows, BLK) for k in range(2)], axis=1)
        return lax.dot_general(
            both, bw[r], (((1,), (1,)), ((), ())), preferred_element_type=jnp.float32
        )

    def couple(w, j):
        both = jnp.concatenate(
            [w[pl.ds(a_at[j][k] * 8, 8)].reshape(BLK, BLK) for k in range(2)], axis=0
        )
        return jnp.dot(aw[j], both, preferred_element_type=jnp.float32)

    def alpha(w, out, rows, more):
        for j in rows:
            product = couple(w, j)
            if more:
                product = product + pre[j]
            out[8 * j : 8 * (j + 1)] = product.astype(jnp.bfloat16).reshape(8, TILE, BLK)

    def alpha_and_send(w, out, rec, step, more):
        alpha(w, out, range(9, 10), more)
        send_far(out, rec, step)
        alpha(w, out, range(6, 9), more)
        send_out(out, rec, step, 1, 2 * PLANE, 0)
        alpha(w, out, range(0, 3), more)
        send_out(out, rec, step, -1, 0, 2)
        alpha(w, out, range(3, 6), more)
        send_own(out, rec, step)

    def send_all(out, rec, step):
        send_far(out, rec, step)
        send_out(out, rec, step, 1, 2 * PLANE, 0)
        send_out(out, rec, step, -1, 0, 2)
        send_own(out, rec, step)

    def returned(rec, cb):
        return jnp.concatenate(
            [rec[slot_at[cb % 2][q], cb, q] for q in range(TILES)], axis=0
        ).astype(jnp.float32)

    for k, (tile, tiles) in enumerate(PARTS):
        rows = slice(TILE * tile, TILE * (tile + tiles))
        y_arrived(yw0[k], k)
        for cb in range(COLB):
            cols = slice(cb * BLK, (cb + 1) * BLK)
            b1 = beta(yw0[k], cb, TILE * tiles).astype(jnp.bfloat16).astype(jnp.float32)
            t = 2.0 * (b1 + dv[rows, cols] * xv[rows, cols]) - pv[rows, cols]
            tv[rows, cols] = t
            yw1[9 + cb, tile : tile + tiles] = t.astype(jnp.bfloat16).reshape(tiles, TILE, BLK)
            tb[k][cb] = (t + 2.0 * b1).astype(jnp.bfloat16).reshape(tiles, TILE, BLK)
        send_in(tb[k], wint, 1, tile, tiles)

    a_table = class_table(acls)
    a_at = []
    for j in range(WIN):
        start, length = class_of(a_block[j], a_table)
        spots = []
        for k in range(2):
            spot = column_of(start, length, aoff[k, a_block[j]], 3) - (z - 1) * ROWB
            spots.append(jnp.where(spot < 0, WIN - 1, jnp.minimum(spot, WIN - 1)))
        a_at.append(spots)
    slot_at = []
    for parity in range(2):
        slots = []
        for q in range(TILES):
            start, length = class_of(z * ROWB + lax.div(TILES * p + q, PLANE), a_table)
            away = lax.div(start + lax.div(length - 1 + parity, 2), ROWB) - z
            slot = jnp.where(jnp.logical_or(away < -1, away > 1), 3, away + 1)
            slots.append(jnp.clip(slot, 0, 3))
        slot_at.append(slots)

    for c in loads[3:]:
        c.wait()

    @pl.when(is_home)
    def _():
        for j in range(WIN):
            for k in range(2):
                live = jnp.full((BLK, BLK), amask[k, a_block[j]].astype(jnp.float32))
                aw[j, :, k * BLK : (k + 1) * BLK] = araw[j, k] * live.astype(jnp.bfloat16)


    y_start(yw1, len(PARTS))

    @pl.when(is_home)
    def _():
        arrived_in(0)
        alpha(win0, al0, range(WIN), False)
        for j in range(WIN):
            pre[j] = 2.0 * couple(al0, j)
        send_all(al0, rec0, 0)
        arrived_in(1)
        alpha_and_send(wint, al1, rec1, 1, True)

    arrived_out(0)
    for cb in range(COLB):
        cols = slice(cb * BLK, (cb + 1) * BLK)
        nv[:, cols] = 2.0 * returned(rec0, cb) + tv[:, cols]
    y_arrived(yw1, len(PARTS))
    for cb in range(COLB):
        cols = slice(cb * BLK, (cb + 1) * BLK)
        tv[:, cols] = 2.0 * (beta(yw1, cb, ROWS) + dv[:, cols] * nv[:, cols]) - xv[:, cols]
    for step in range(2):
        sent_in(step)
        pl.when(is_home)(lambda step=step: sent_out(step))
    for k in range(len(PARTS)):
        y_sent(yw0[k], k)
    y_sent(yw1, len(PARTS))
    arrived_out(1)
    for cb in range(COLB):
        cols = slice(cb * BLK, (cb + 1) * BLK)
        ov[:, cols] = tv[:, cols] + 2.0 * returned(rec1, cb)


def hand_over(next_in, after_in, next_out, after_out, sem):
    copies = [
        pltpu.make_async_copy(next_in, next_out, sem.at[0]),
        pltpu.make_async_copy(after_in, after_out, sem.at[1]),
    ]
    for c in copies:
        c.start()
    for c in copies:
        c.wait()


def on_device(prev, this, diag, ablk, acls, aoff, amask, bblk, bcls, boff, bmask):
    rows, columns = ROWS, COLB * BLK
    f32, bf16 = jnp.float32, jnp.bfloat16
    hbm = pl.BlockSpec(memory_space=pltpu.HBM)
    vmem = pl.BlockSpec(memory_space=pltpu.VMEM)
    smem = pl.BlockSpec(memory_space=pltpu.SMEM)
    dma = pltpu.SemaphoreType.DMA
    next_vector, after_vector = pl.pallas_call(
        kernel,
        out_shape=[pltpu.VMEM((rows, columns), f32)] * 2,
        in_specs=[hbm, hbm, hbm, hbm, smem, smem, smem, hbm, smem, smem, smem],
        out_specs=[vmem, vmem],
        scratch_shapes=[
            *[pltpu.VMEM((rows, columns), f32)] * 4,
            pltpu.VMEM((COLB, TILES, TILE, BLK), bf16),
            pltpu.VMEM((YWIN, TILES, TILE, BLK), bf16),
            pltpu.VMEM((WIN, BLK, BLK), f32),
            *[pltpu.VMEM((WIN * BTILES, TILE, BLK), bf16)] * 4,
            *[pltpu.VMEM((4, COLB, TILES, TILE, BLK), bf16)] * 2,
            pltpu.VMEM((WIN, 2, BLK, BLK), bf16),
            pltpu.VMEM((COLB, 2, BLK, BLK), bf16),
            pltpu.VMEM((WIN, BLK, 2 * BLK), bf16),
            pltpu.VMEM((COLB, BLK, 2 * BLK), bf16),
            dma((8,)),
            dma((TILES,)),
            *[dma((2, 4))] * 4,
            dma((1 + len(PARTS), 2, 4)),
            dma((4,)),
            *[pltpu.VMEM((YWIN, tiles, TILE, BLK), bf16) for _, tiles in PARTS],
            *[pltpu.VMEM((COLB, tiles, TILE, BLK), bf16) for _, tiles in PARTS],
        ],
        compiler_params=pltpu.CompilerParams(
            collective_id=0, has_side_effects=True, vmem_limit_bytes=60 * 1024 * 1024
        ),
        name="chebyshev_steps",
    )(prev, this, diag, ablk, acls, aoff.T, amask.T, bblk, bcls, boff.T, bmask.T)
    return pl.pallas_call(
        hand_over,
        out_shape=[jax.ShapeDtypeStruct((rows, columns), f32)] * 2,
        in_specs=[pl.BlockSpec(memory_space=pl.ANY)] * 2,
        out_specs=[hbm, hbm],
        scratch_shapes=[dma((2,))],
        compiler_params=pltpu.CompilerParams(vmem_limit_bytes=1024 * 1024),
        name="hand_over",
    )(next_vector, after_vector)


def solution(mesh):
    own = P("aa", "ba")
    return jax.shard_map(
        on_device,
        mesh=mesh,
        in_specs=(own, own, own, *[P()] * 8),
        out_specs=(own, own),
        check_vma=False,
    )
```
